32 devices in a mesh: ctx: 8 (over z, x), ch: 4 (over y, core).
Axes of the slice: x: 2, y: 2, z: 4, core: 2. Of those that a mesh axis runs over, the one named last changes fastest.
Arguments:
- signal: bfloat16 [4096, 1024], P('ctx', 'ch'), may hold values from -6 to 6
- gate_v: bfloat16 [4096, 1024], P('ctx', 'ch'), may hold values from -6 to 6
- taps: float32 [4096, 1024], P('ctx', 'ch'), may hold values from -1 to 1
- skip: float32 [1024], P('ch'), may hold values from -1 to 1
- norm_gain: float32 [1024], replicated, may hold values from 0.5 to 1.5
- router: float32 [1024, 32], replicated, may hold values from -0.1875 to 0.1875
- w_up: bfloat16 [64, 1024, 256], P('ctx'), may hold values from -0.1875 to 0.1875
- w_down: bfloat16 [64, 256, 1024], P('ctx'), may hold values from -0.25 to 0.25
- routes: int32 [4096, 2], P(('ctx', 'ch')), may hold values from 0 to 31, all different within a row; in each aligned block of 128 rows (0 to 127, 128 to 255, ...) at most 16 rows name the same one
Outputs:
- mixed: bfloat16 [4096, 1024], P('ctx', 'ch')
- moe_out: bfloat16 [4096, 1024], P('ctx', 'ch')
The draws below stay inside these ranges and needn't reach their ends.
Inputs may be any that keep to these rules, and one draw needn't show every extreme that they name: `routes`: each row names two different experts. In each aligned block of 128 rows no expert is named by more than 16 rows.
All inputs are finite; a program needn't handle non-finite values.
Results may differ from the reference program's by a relative error of at most 0.017.
Values may be sent and summed in bfloat16 or wider, within the bound.
No kernel may reach another device: no remote copies, remote signals or barrier semaphores. Data moves between devices by JAX's collectives and lax.ppermute only.
A program may use at most 64 MiB of HBM per device.

```python
import math
import jax
import jax.numpy as jnp
import numpy as np
from jax import lax

D = 1024
HID = 512
EXPERTS = 32
CAP = 16
HALF = 256
PARTS_SIZE = 64
TOKENS = 4096
ROWS_EX = 128


def draw_taps(key, part):
    key_noise, key_rate = jax.random.split(jax.random.fold_in(key, 17))
    steps = jnp.arange(TOKENS, dtype=jnp.float32)[:, None]
    length = jnp.exp(jax.random.uniform(key_rate, (1, D), jnp.float32, math.log(40.0), math.log(4.0 * TOKENS)))
    noise = jax.random.truncated_normal(key_noise, -4.0, 4.0, (TOKENS, D), jnp.float32)
    ratio = jnp.exp(-1.0 / length)
    scale = jnp.sqrt((1.0 - ratio * ratio) / (1.0 - jnp.exp(-2.0 * TOKENS / length)))
    return noise * scale * jnp.exp(-steps / length)


def level_of(rng, dims, shards, least, high):
    gain, own = 1.0, jax.random.fold_in(rng, 6)
    for axis_at, blocks in shards:
        steps = jnp.exp(jax.random.uniform(jax.random.fold_in(own, axis_at), (blocks,), jnp.float32, least / len(shards), high / len(shards)))
        gain = gain * jnp.repeat(steps, dims[axis_at] // blocks).reshape([-1 if axis == axis_at else 1 for axis in range(len(dims))])
    return gain


def assign_block(own_key, own, number, rows, count, top, most, skew):
    sequence = jax.random.permutation(own_key, count)
    packed, common = portions_of(count, rows * top, most, skew, True), portions_of(count, rows * top, most, skew, False)
    places = jnp.arange(count)

    def named(sizes, rotation):
        used = int((sizes > 0).sum())
        fixed = max(1, used // 4)
        shifted = fixed + (places - fixed + rotation * (used - fixed)) % max(1, count - fixed)
        return jnp.zeros((count,), jnp.int32).at[sequence[jnp.where(places < fixed, places, shifted)]].set(jnp.asarray(sizes, jnp.int32))

    sizes = jnp.where(number % 4 == 0, named(packed, number // 4), named(common, number - number // 4 - 1))
    mixed = jax.random.permutation(jax.random.fold_in(own, 3), count)
    donor, sink = mixed[0:count // 2 * 2:2], mixed[1:count // 2 * 2:2]
    room = jnp.minimum(sizes[donor] - 1, most - sizes[sink]) // 2
    room = jnp.where((donor == sequence[0]) | (sink == sequence[0]) | (sizes[sink] == 0), 0, jnp.maximum(room, 0))
    shifted = jax.random.randint(jax.random.fold_in(own, 4), (count // 2,), 0, 1 << 20) % (room + 1)
    sizes = sizes.at[donor].add(-shifted).at[sink].add(shifted)
    members = jnp.searchsorted(jnp.cumsum(sizes), jnp.arange(rows * top), side="right").astype(jnp.int32)
    grid = members.reshape(top, rows).T
    grid = grid[jax.random.permutation(jax.random.fold_in(own, 1), rows)]
    rotation = jax.random.randint(jax.random.fold_in(own, 2), (rows, 1), 0, top)
    return jnp.take_along_axis(grid, (jnp.arange(top)[None, :] + rotation) % top, axis=1)


def portions_of(amount, total, most, slope, full):
    loads = [(1 << 20) // math.isqrt(rank ** slope) + 1 for rank in range(1, amount + 1)]
    largest = most if full else min(most, max(-(-total // amount), total * loads[0] // sum(loads)))
    least = 1 if total - largest >= amount - 1 else 0
    given, surplus = [largest] + [least] * (amount - 1), total - largest - least * (amount - 1)
    while surplus > 0:
        free = [i for i in range(1, amount) if given[i] < largest] or [i for i in range(1, amount) if given[i] < most]
        mass, left = sum([loads[i] for i in free]), surplus
        for i in free:
            extra = min(most - given[i], max(1, left * loads[i] // mass), surplus)
            given[i] = given[i] + extra
            surplus = surplus - extra
    return np.array(given)


def centred(key, dims, spread, reach, cuts=(), kind=jnp.bfloat16):
    result = spread * jax.random.normal(key, dims, jnp.float32)
    if cuts:
        result = result * level_of(key, dims, cuts, -0.22, 0.18)
    return jnp.clip(result, -reach, reach).astype(kind)


def setup_inputs(seed: int = 0) -> dict:
    keys = jax.random.split(jax.random.key(seed), 10)
    signal = centred(keys[0], (TOKENS, D), 1.0, 6.0, ((0, 8), (1, 4)))
    gate_v = centred(keys[1], (TOKENS, D), 1.0, 6.0, ((0, 8), (1, 4)))
    taps = draw_taps(jax.random.fold_in(keys[9], 71), 0)
    skip = jnp.clip(jax.random.uniform(keys[3], (D,), jnp.float32, -1.0, 1.0) * level_of(keys[3], (D,), ((0, 4),), -0.4, 0.0), -1.0, 1.0)
    norm_gain = jnp.clip(1.0 + 0.1 * jax.random.normal(keys[4], (D,), jnp.float32), 0.5, 1.5)
    router = centred(keys[5], (D, EXPERTS), D ** -0.5, 0.1875, (), jnp.float32)
    w_up = centred(keys[6], (PARTS_SIZE, D, HALF), D ** -0.5, 0.1875, ((0, 8),))
    w_down = centred(keys[7], (PARTS_SIZE, HALF, D), HID ** -0.5, 0.25, ((0, 8),))
    routes_keys = jax.random.split(jax.random.fold_in(keys[8], 1), TOKENS // ROWS_EX)
    routes_turns = jax.random.permutation(jax.random.fold_in(keys[8], 3), TOKENS // ROWS_EX)
    routes = jax.vmap(lambda own, number: assign_block(jax.random.fold_in(keys[8], 2), own, number, ROWS_EX, EXPERTS, 2, CAP, 2))(routes_keys, routes_turns).reshape((TOKENS, 2))
    return dict(signal=signal, gate_v=gate_v, taps=taps, skip=skip, norm_gain=norm_gain, router=router, w_up=w_up, w_down=w_down, routes=routes)


def reference(signal, gate_v, taps, skip, norm_gain, router, w_up, w_down, routes):
    total = signal.shape[0]
    width = signal.shape[1]
    sig_float = signal.astype(jnp.float32)
    spec_sig = jnp.fft.rfft(sig_float, n=2 * total, axis=0)
    spec_tap = jnp.fft.rfft(taps, n=2 * total, axis=0)
    conv = jnp.fft.irfft(spec_sig * spec_tap, n=2 * total, axis=0)[:total].astype(jnp.float32)
    mixed = (gate_v.astype(jnp.float32) * (conv + skip * sig_float)).astype(jnp.bfloat16)
    rows_float = mixed.astype(jnp.float32)
    scale_row = lax.rsqrt(lax.optimization_barrier(jnp.mean(rows_float * rows_float, axis=-1, keepdims=True)) + 1e-05)
    normed = (rows_float * scale_row * norm_gain).astype(jnp.bfloat16)
    logits = jnp.dot(normed.astype(jnp.float32), router, precision=lax.Precision.HIGHEST)
    gates = jax.nn.sigmoid(jnp.take_along_axis(logits, routes, axis=1))
    nblock = total // ROWS_EX
    flat = routes.reshape(nblock, 2 * ROWS_EX)
    onehot = (flat[:, :, None] == jnp.arange(EXPERTS, dtype=jnp.int32)[None, None, :]).astype(jnp.int32)
    slot_of = lax.optimization_barrier(jnp.sum((jnp.cumsum(onehot, axis=1) - onehot) * onehot, axis=-1)).astype(jnp.int32)
    token_of = (jnp.arange(total * 2, dtype=jnp.int32) // 2).reshape(nblock, 2 * ROWS_EX)
    target = flat * (nblock * CAP) + jnp.arange(nblock, dtype=jnp.int32)[:, None] * CAP + slot_of
    target = target.reshape(-1).astype(jnp.int32)
    table = jnp.full((EXPERTS * nblock * CAP,), total, jnp.int32).at[target].set(token_of.reshape(-1))
    gate_table = jnp.zeros((EXPERTS * nblock * CAP,), jnp.float32).at[target].set(gates.reshape(-1))
    table = table.reshape(EXPERTS, nblock * CAP)
    gate_table = gate_table.reshape(EXPERTS, nblock * CAP)
    padded = jnp.concatenate([normed, jnp.zeros((1, width), jnp.bfloat16)], axis=0)
    up_pairs = w_up.reshape(EXPERTS, 2, width, HALF)
    down_pairs = w_down.reshape(EXPERTS, 2, HALF, width)

    def expert_step(accum, inputs):
        index_rows, gate_rows, up_pair, down_pair = inputs
        chosen = padded[index_rows]
        summed = jnp.zeros((chosen.shape[0], width), jnp.float32)
        for half in range(2):
            hidden = jax.nn.gelu(jnp.dot(chosen, up_pair[half], preferred_element_type=jnp.float32), approximate=True).astype(jnp.bfloat16)
            part = jnp.dot(hidden, down_pair[half], preferred_element_type=jnp.float32).astype(jnp.bfloat16)
            summed = summed + part.astype(jnp.float32)
        accum = accum.at[index_rows].add(gate_rows[:, None] * summed)
        return (accum, None)
    start = jnp.zeros((total + 1, width), jnp.float32)
    accum, unused = lax.scan(expert_step, start, (table, gate_table, up_pairs, down_pairs))
    moe_out = accum[:total].astype(jnp.bfloat16)
    return (mixed, moe_out)
```

```python
import functools
import math

import jax
import jax.numpy as jnp
import ml_dtypes
import numpy as np
from jax import lax
from jax.experimental import pallas as pl
from jax.experimental.pallas import tpu as pltpu
from jax.sharding import PartitionSpec as P

CAP = 16
SKIP_ROWS = 16
VMEM_LIMIT = 48 * 1024 * 1024

f32 = jnp.float32
bf16 = jnp.bfloat16


def params(limit=VMEM_LIMIT):
    return pltpu.CompilerParams(vmem_limit_bytes=limit)


def call(kernel, out_shape, scalars, operands, name, scratch=(), cost=None):
    vmem = pl.BlockSpec(memory_space=pltpu.VMEM)
    smem = pl.BlockSpec(memory_space=pltpu.SMEM)
    return pl.pallas_call(
        kernel,
        out_shape=out_shape,
        in_specs=[smem] * len(scalars) + [vmem] * len(operands),
        out_specs=jax.tree.map(lambda _: vmem, out_shape),
        scratch_shapes=scratch,
        compiler_params=params(),
        cost_estimate=cost,
        name=name,
    )(*scalars, *operands)


def cmul(a, w):
    re, im = a
    wr, wi = w.real, w.imag
    if abs(wi) < 1e-12:
        return (re, im) if wr > 0 else (-re, -im)
    if abs(wr) < 1e-12:
        return (-im, re) if wi > 0 else (im, -re)
    return (re * wr - im * wi, re * wi + im * wr)


def fft(values, sign):
    count = len(values)
    if count == 1:
        return values
    even, odd = fft(values[::2], sign), fft(values[1::2], sign)
    low, high = [], []
    for k in range(count // 2):
        angle = sign * 2.0 * math.pi * k / count
        tr, ti = cmul(odd[k], complex(math.cos(angle), math.sin(angle)))
        er, ei = even[k]
        low.append((er + tr, ei + ti))
        high.append((er - tr, ei - ti))
    return low + high


def tables(shards, length):
    index = np.arange(length)
    angle = 2.0 * np.pi / length * (np.outer(index, index) % length)
    turn = 2.0 * np.pi / (shards * length) * np.outer(np.arange(shards) + 0.25, index)
    narrow = ml_dtypes.bfloat16
    return (
        np.cos(angle).astype(narrow),
        np.sin(angle).astype(narrow),
        np.cos(turn).astype(np.float32),
        np.sin(turn).astype(np.float32),
    )


def prep_kernel(groups, blocks, me, sig, gate, taps, skip, spread, *pieces):
    tok, chans = sig.shape
    per = chans // groups
    sig_t = sig[...].astype(f32).T.astype(bf16)
    tap_t = taps[...].T.astype(bf16)
    for g in range(groups):
        spread[g, :per, :] = sig_t[g * per : (g + 1) * per, :]
        spread[g, per:, :] = tap_t[g * per : (g + 1) * per, :]
    rows = tok // blocks
    own = skip[...]
    first = own.astype(bf16)
    own = own - first.astype(f32)
    second = own.astype(bf16)
    third = (own - second.astype(f32)).astype(bf16)
    row = lax.broadcasted_iota(jnp.int32, (SKIP_ROWS, chans), 0)
    wide = jnp.where(
        row == 0,
        first.astype(f32),
        jnp.where(
            row == 1, second.astype(f32), jnp.where(row == 2, third.astype(f32), 0.0)
        ),
    ).astype(bf16)
    for o in range(blocks):
        start = pl.multiple_of((me[0] ^ o) * rows, rows)
        pieces[o][:rows, :] = gate[pl.ds(start, rows), :]
        pieces[o][rows : 2 * rows, :] = sig[pl.ds(start, rows), :]
        pieces[o][2 * rows :, :] = wide


def conv_kernel(blocks, got, cos, sin, turn_cos, turn_sin, out, are, aim, pre, pim):
    shards, twice, tok = got.shape
    per = twice // 2
    rows = tok // blocks
    step = min(per, 16)
    total = shards * tok
    half = shards * per
    twist = [
        complex(math.cos(0.5 * math.pi * j / shards), math.sin(0.5 * math.pi * j / shards))
        for j in range(shards)
    ]
    for which in range(2):
        for r in range(0, per, step):
            for b in range(blocks):
                lanes = slice(b * rows, (b + 1) * rows)
                values = []
                for j in range(shards):
                    x = got[j, which * per + r : which * per + r + step, lanes].astype(f32)
                    values.append((x * twist[j].real, x * -twist[j].imag))
                for k, (re, im) in enumerate(fft(values, -1.0)):
                    c, s = turn_cos[k : k + 1, lanes], turn_sin[k : k + 1, lanes]
                    at = which * half + k * per + r
                    are[at : at + step, lanes] = (re * c + im * s).astype(bf16)
                    aim[at : at + step, lanes] = (im * c - re * s).astype(bf16)

    def dot(a, b):
        return jnp.dot(a, b, preferred_element_type=f32)

    xr = dot(are[...], cos[...]) + dot(aim[...], sin[...])
    xi = dot(aim[...], cos[...]) - dot(are[...], sin[...])
    sr, hr, si, hi = xr[:half], xr[half:], xi[:half], xi[half:]
    prod_re = (sr * hr - si * hi).astype(bf16)
    prod_im = (sr * hi + si * hr).astype(bf16)
    pre[...] = dot(prod_re, cos[...]) - dot(prod_im, sin[...])
    pim[...] = dot(prod_im, cos[...]) + dot(prod_re, sin[...])
    for r in range(0, per, step):
        for b in range(blocks):
            lanes = slice(b * rows, (b + 1) * rows)
            values = []
            for k in range(shards):
                c, s = turn_cos[k : k + 1, lanes], turn_sin[k : k + 1, lanes]
                at = k * per + r
                re, im = pre[at : at + step, lanes], pim[at : at + step, lanes]
                values.append((re * c - im * s, im * c + re * s))
            for j, (re, im) in enumerate(fft(values, 1.0)):
                y = (re * twist[j].real - im * twist[j].imag) * (1.0 / total)
                out[j, b, r : r + step, :] = y.astype(bf16)


def slots(routes_t, experts):
    rows = routes_t.shape[1]
    expert = lax.broadcasted_iota(jnp.int32, (experts, rows), 0)
    named = [routes_t[k : k + 1, :] == expert for k in range(2)]
    either = jnp.where(named[0] | named[1], 1.0, 0.0).astype(bf16)
    before = lax.broadcasted_iota(jnp.int32, (rows, rows), 0)
    after = lax.broadcasted_iota(jnp.int32, (rows, rows), 1)
    ahead = jnp.where(before < after, 1.0, 0.0).astype(bf16)
    rank = jnp.dot(either, ahead, preferred_element_type=f32).astype(jnp.int32)
    slot = lax.broadcasted_iota(jnp.int32, (experts, CAP, rows), 1)
    picks = []
    for k in range(2):
        mine = jnp.where(named[k], rank, -1)
        picks.append(jnp.where(mine[:, None, :] == slot, 1.0, 0.0))
    return picks


def rows_kernel(experts, blocks, me, routes_t, gain, conv, *refs):
    pieces, refs = refs[:blocks], refs[blocks:]
    mixed_out, (send, normed_out, mixed) = refs[:blocks], refs[blocks:]
    shards, _, per, rows = conv.shape
    chans = shards * per
    width = chans * blocks
    square = jnp.zeros((rows, 1), f32)
    for o in range(blocks):
        group = me[0] ^ o
        piece = pieces[o]
        gate = piece[:rows, :].astype(f32)
        sig = piece[rows : 2 * rows, :].astype(f32)
        skip = piece[2 * rows :, :].astype(f32)
        skip = skip[0:1, :] + skip[1:2, :] + skip[2:3, :]
        y = conv[:, group, :, :].astype(f32).reshape(chans, rows).T
        value = (gate * (y + skip * sig)).astype(bf16)
        mixed[group] = value
        mixed_out[o][...] = value
        value = value.astype(f32)
        square = square + jnp.sum(value * value, axis=1, keepdims=True)
    scale = lax.rsqrt(square * (1.0 / width) + 1e-05)
    for h in range(blocks):
        lanes = slice(h * chans, (h + 1) * chans)
        normed_out[:, lanes] = (mixed[h].astype(f32) * scale * gain[:, lanes]).astype(bf16)
    first, second = slots(routes_t[...], experts)
    pick = (first + second).astype(bf16).reshape(experts * CAP, rows)
    sent = jnp.dot(pick, normed_out[...], preferred_element_type=f32).astype(bf16)
    count, size, _ = send.shape
    copies = count * size // (experts * CAP)
    if copies == 1:
        send[...] = sent.reshape(count, size, width)
    else:
        for p in range(count):
            e = p // copies
            send[p] = sent[e * CAP : (e + 1) * CAP, :]


def gates_kernel(normed, router, routes, gates):
    logits = jnp.dot(
        normed[...].astype(f32),
        router[...],
        precision=lax.Precision.HIGHEST,
        preferred_element_type=f32,
    )
    expert = lax.broadcasted_iota(jnp.int32, logits.shape, 1)
    for k in range(2):
        picked = jnp.where(routes[:, k : k + 1] == expert, logits, 0.0)
        value = jnp.sum(picked, axis=1, keepdims=True)
        gates[:, k : k + 1] = jax.nn.sigmoid(value)


def expert_kernel(got, up, down, out):
    shards, size, width = got.shape
    parts = up.shape[0]
    x = got[...].reshape(shards * size, width)
    total = jnp.zeros((shards * size, width), f32)
    for p in range(parts):
        hidden = jnp.dot(x, up[p], preferred_element_type=f32)
        hidden = jax.nn.gelu(hidden, approximate=True).astype(bf16)
        total = total + jnp.dot(hidden, down[p], preferred_element_type=f32)
    out[...] = total.astype(bf16).reshape(shards, size, width)


def combine_kernel(experts, blocks, me, routes_t, gates, back, *out):
    count, size, width = back.shape
    rows = routes_t.shape[1]
    chans = width // blocks
    copies = count * size // (experts * CAP)
    picks = slots(routes_t[...], experts)
    total = jnp.zeros((rows, width), f32)
    for k in range(2):
        pick = picks[k].astype(bf16).reshape(experts * CAP, rows)
        for c in range(copies):
            if copies == 1:
                values = back[...].reshape(experts * CAP, width)
            else:
                values = jnp.concatenate([back[e * copies + c] for e in range(experts)], axis=0)
            chosen = lax.dot_general(
                pick, values, (((0,), (0,)), ((), ())), preferred_element_type=f32
            )
            total = total + gates[:, k : k + 1] * chosen
    total = total.astype(bf16)
    for h in range(blocks):
        out[0][h] = total[:, h * chans : (h + 1) * chans]


def place_kernel(me, *refs):
    pieces, out = refs[:-1], refs[-1]
    rows = pieces[0].shape[0]
    for o, piece in enumerate(pieces):
        start = pl.multiple_of((me[0] ^ o) * rows, rows)
        out[pl.ds(start, rows), :] = piece[...]


def swap(pieces, axis):
    count = len(pieces)
    return [pieces[0]] + [
        lax.ppermute(pieces[o], axis, [(i, i ^ o) for i in range(count)]) for o in range(1, count)
    ]


def body(signal, gate_v, taps, skip, norm_gain, router, w_up, w_down, routes):
    tok, chans = signal.shape
    shards, blocks = lax.axis_size("ctx"), lax.axis_size("ch")
    per, rows, width = chans // shards, tok // blocks, chans * blocks
    experts = router.shape[1]
    parts = w_up.shape[0]
    owned = max(1, parts // 2)
    me = lax.axis_index("ch").astype(jnp.int32).reshape(1)
    shape = jax.ShapeDtypeStruct

    spread, *pieces = call(
        functools.partial(prep_kernel, shards, blocks),
        [shape((shards, 2 * per, tok), bf16)] + [shape((2 * rows + SKIP_ROWS, chans), bf16)] * blocks,
        [me],
        [signal, gate_v, taps, skip.reshape(1, chans)],
        "prep",
    )
    pieces = swap(pieces, "ch")
    got = lax.all_to_all(spread, "ctx", split_axis=0, concat_axis=0, tiled=True)
    conv = call(
        functools.partial(conv_kernel, blocks),
        shape((shards, blocks, per, rows), bf16),
        [],
        [got, *tables(shards, tok)],
        "conv",
        [pltpu.VMEM((2 * shards * per, tok), bf16)] * 2 + [pltpu.VMEM((shards * per, tok), f32)] * 2,
    )
    conv = lax.all_to_all(
        conv.reshape(shards * blocks, per, rows), ("ctx", "ch"), split_axis=0, concat_axis=0, tiled=True
    ).reshape(shards, blocks, per, rows)
    routes_t = routes.T
    *mixed, send, normed = call(
        functools.partial(rows_kernel, experts, blocks),
        [shape((rows, chans), bf16)] * blocks
        + [shape((shards, owned * CAP, width), bf16), shape((rows, width), bf16)],
        [me],
        [routes_t, norm_gain.reshape(1, width), conv, *pieces],
        "rows",
        [pltpu.VMEM((blocks, rows, chans), bf16)],
    )
    mixed = swap(mixed, "ch")
    there = lax.all_to_all(send, "ctx", split_axis=0, concat_axis=0, tiled=True)
    gates = call(gates_kernel, shape((rows, 2), f32), [], [normed, router, routes], "gates")
    mixed = call(place_kernel, shape((tok, chans), bf16), [me], mixed, "place")
    group = min(parts, 2)
    size = owned * CAP
    result = pl.pallas_call(
        expert_kernel,
        grid=(owned,),
        out_shape=shape((shards, size, width), bf16),
        in_specs=[
            pl.BlockSpec((shards, CAP, width), lambda e: (0, e, 0)),
            pl.BlockSpec((group,) + w_up.shape[1:], lambda e: (e, 0, 0)),
            pl.BlockSpec((group,) + w_down.shape[1:], lambda e: (e, 0, 0)),
        ],
        out_specs=pl.BlockSpec((shards, CAP, width), lambda e: (0, e, 0)),
        compiler_params=params(),
        name="experts",
    )(there, w_up, w_down)
    back = lax.all_to_all(result, "ctx", split_axis=0, concat_axis=0, tiled=True)
    (moe_rows,) = call(
        functools.partial(combine_kernel, experts, blocks),
        [shape((blocks, rows, chans), bf16)],
        [me],
        [routes_t, gates, back],
        "combine",
    )
    moe_out = lax.all_to_all(moe_rows, "ch", split_axis=0, concat_axis=0, tiled=True)
    return (mixed, moe_out.reshape(tok, chans))


def solution(mesh):
    in_specs = (
        P("ctx", "ch"),
        P("ctx", "ch"),
        P("ctx", "ch"),
        P("ch"),
        P(),
        P(),
        P("ctx", None, None),
        P("ctx", None, None),
        P(("ctx", "ch"), None),
    )
    out_specs = (P("ctx", "ch"), P("ctx", "ch"))
    return jax.shard_map(body, mesh=mesh, in_specs=in_specs, out_specs=out_specs, check_vma=False)
```

```python
import functools
import math

import jax
import jax.numpy as jnp
from jax import lax
from jax.experimental import pallas as pl
from jax.experimental.pallas import tpu as pltpu
from jax.sharding import PartitionSpec as P

CAP = 16
SKIP_ROWS = 16
VMEM_LIMIT = 40 * 1024 * 1024
PREP_LIMIT = 62 * 1024 * 1024

f32 = jnp.float32
bf16 = jnp.bfloat16


def params(limit=VMEM_LIMIT):
    return pltpu.CompilerParams(vmem_limit_bytes=limit)


def call(kernel, out_shape, scalars, far, operands, name, scratch=(), limit=VMEM_LIMIT):
    vmem = pl.BlockSpec(memory_space=pltpu.VMEM)
    smem = pl.BlockSpec(memory_space=pltpu.SMEM)
    hbm = pl.BlockSpec(memory_space=pltpu.HBM)
    if far:
        held = [pltpu.VMEM(x.shape, x.dtype) for x in far]
        scratch = [*scratch, *held, pltpu.SemaphoreType.DMA((len(far),))]
    return pl.pallas_call(
        kernel,
        out_shape=out_shape,
        in_specs=[smem] * len(scalars) + [hbm] * len(far) + [vmem] * len(operands),
        out_specs=jax.tree.map(lambda _: vmem, out_shape),
        scratch_shapes=scratch,
        compiler_params=params(limit),
        name=name,
    )(*scalars, *far, *operands)


def fetch(far, held, sems):
    copies = [pltpu.make_async_copy(a, b, sems.at[i]) for i, (a, b) in enumerate(zip(far, held))]
    for copy in copies:
        copy.start()
    return copies


def cmul(a, w):
    re, im = a
    wr, wi = w.real, w.imag
    if abs(wi) < 1e-12:
        return (re, im) if wr > 0 else (-re, -im)
    if abs(wr) < 1e-12:
        return (-im, re) if wi > 0 else (im, -re)
    return (re * wr - im * wi, re * wi + im * wr)


def fft(values, sign):
    count = len(values)
    if count == 1:
        return values
    even, odd = fft(values[::2], sign), fft(values[1::2], sign)
    low, high = [], []
    for k in range(count // 2):
        angle = sign * 2.0 * math.pi * k / count
        tr, ti = cmul(odd[k], complex(math.cos(angle), math.sin(angle)))
        er, ei = even[k]
        low.append((er + tr, ei + ti))
        high.append((er - tr, ei - ti))
    return low + high


def tables_kernel(turn_cos, turn_sin, cos, sin, wide_cos, wide_sin):
    shards, length = turn_cos.shape
    shape = (shards, length)
    shard = lax.broadcasted_iota(jnp.int32, shape, 0).astype(f32) + 0.25
    lane = lax.broadcasted_iota(jnp.int32, shape, 1).astype(f32)
    angle = shard * lane * (2.0 * math.pi / (shards * length))
    turn_cos[...] = jnp.cos(angle)
    turn_sin[...] = jnp.sin(angle)
    row = lax.broadcasted_iota(jnp.int32, (8, length), 0)
    lane = lax.broadcasted_iota(jnp.int32, (8, length), 1)
    angle = ((row * lane) & (length - 1)).astype(f32) * (2.0 * math.pi / length)
    wide_cos[0:8, :] = jnp.cos(angle)
    wide_sin[0:8, :] = jnp.sin(angle)
    angle = ((lane << (row + 3)) & (length - 1)).astype(f32) * (2.0 * math.pi / length)
    step_cos, step_sin = jnp.cos(angle), jnp.sin(angle)
    count = 8
    for level in range((length // 8).bit_length() - 1):
        c, s = step_cos[level : level + 1, :], step_sin[level : level + 1, :]
        have_cos, have_sin = wide_cos[0:count, :], wide_sin[0:count, :]
        wide_cos[count : 2 * count, :] = have_cos * c - have_sin * s
        wide_sin[count : 2 * count, :] = have_sin * c + have_cos * s
        count = 2 * count
    cos[...] = wide_cos[...].astype(bf16)
    sin[...] = wide_sin[...].astype(bf16)


def prep_kernel(groups, blocks, me, *refs):
    far, refs = refs[:4], refs[4:]
    spread, pieces, held, sems = refs[0], refs[1 : 1 + blocks], refs[1 + blocks : -1], refs[-1]
    copies = fetch(far, held, sems)
    sig, taps, gate, skip = held
    tok, chans = sig.shape
    per = chans // groups
    copies[0].wait()
    sig_t = sig[...].astype(f32).T.astype(bf16)
    for g in range(groups):
        spread[g, :per, :] = sig_t[g * per : (g + 1) * per, :]
    copies[1].wait()
    tap_t = taps[...].T.astype(bf16)
    for g in range(groups):
        spread[g, per:, :] = tap_t[g * per : (g + 1) * per, :]
    copies[2].wait()
    copies[3].wait()
    rows = tok // blocks
    own = skip[...]
    first = own.astype(bf16)
    own = own - first.astype(f32)
    second = own.astype(bf16)
    third = (own - second.astype(f32)).astype(bf16)
    row = lax.broadcasted_iota(jnp.int32, (SKIP_ROWS, chans), 0)
    wide = jnp.zeros((SKIP_ROWS, chans), f32)
    for i, term in enumerate((first, second, third)):
        wide = jnp.where(row == i, term.astype(f32), wide)
    wide = wide.astype(bf16)
    for o in range(blocks):
        start = pl.multiple_of((me[0] ^ o) * rows, rows)
        pieces[o][:rows, :] = gate[pl.ds(start, rows), :]
        pieces[o][rows : 2 * rows, :] = sig[pl.ds(start, rows), :]
        pieces[o][2 * rows :, :] = wide


def conv_kernel(blocks, got, turn_cos, turn_sin, cos, sin, out, are, aim, pre, pim):
    shards, twice, tok = got.shape
    per = twice // 2
    rows = tok // blocks
    step = min(per, 16)
    total = shards * tok
    half = shards * per
    twist = [
        complex(math.cos(0.5 * math.pi * j / shards), math.sin(0.5 * math.pi * j / shards))
        for j in range(shards)
    ]
    for which in range(2):
        for r in range(0, per, step):
            for b in range(blocks):
                lanes = slice(b * rows, (b + 1) * rows)
                values = []
                for j in range(shards):
                    x = got[j, which * per + r : which * per + r + step, lanes].astype(f32)
                    values.append((x * twist[j].real, x * -twist[j].imag))
                for k, (re, im) in enumerate(fft(values, -1.0)):
                    c, s = turn_cos[k : k + 1, lanes], turn_sin[k : k + 1, lanes]
                    at = which * half + k * per + r
                    are[at : at + step, lanes] = (re * c + im * s).astype(bf16)
                    aim[at : at + step, lanes] = (im * c - re * s).astype(bf16)

    def dot(a, b):
        return jnp.dot(a, b, preferred_element_type=f32)

    xr = dot(are[...], cos[...]) + dot(aim[...], sin[...])
    xi = dot(aim[...], cos[...]) - dot(are[...], sin[...])
    sr, hr, si, hi = xr[:half], xr[half:], xi[:half], xi[half:]
    prod_re = (sr * hr - si * hi).astype(bf16)
    prod_im = (sr * hi + si * hr).astype(bf16)
    pre[...] = dot(prod_re, cos[...]) - dot(prod_im, sin[...])
    pim[...] = dot(prod_im, cos[...]) + dot(prod_re, sin[...])
    for r in range(0, per, step):
        for b in range(blocks):
            lanes = slice(b * rows, (b + 1) * rows)
            values = []
            for k in range(shards):
                c, s = turn_cos[k : k + 1, lanes], turn_sin[k : k + 1, lanes]
                at = k * per + r
                re, im = pre[at : at + step, lanes], pim[at : at + step, lanes]
                values.append((re * c - im * s, im * c + re * s))
            for j, (re, im) in enumerate(fft(values, 1.0)):
                y = (re * twist[j].real - im * twist[j].imag) * (1.0 / total)
                out[j, b, r : r + step, :] = y.astype(bf16)


def slots(routes_t, experts):
    rows = routes_t.shape[1]
    expert = lax.broadcasted_iota(jnp.int32, (experts, rows), 0)
    named = [routes_t[k : k + 1, :] == expert for k in range(2)]
    either = jnp.where(named[0] | named[1], 1.0, 0.0).astype(bf16)
    before = lax.broadcasted_iota(jnp.int32, (rows, rows), 0)
    after = lax.broadcasted_iota(jnp.int32, (rows, rows), 1)
    ahead = jnp.where(before < after, 1.0, 0.0).astype(bf16)
    rank = jnp.dot(either, ahead, preferred_element_type=f32).astype(jnp.int32)
    slot = lax.broadcasted_iota(jnp.int32, (experts, CAP, rows), 1)
    picks = []
    for k in range(2):
        mine = jnp.where(named[k], rank, -1)
        picks.append(jnp.where(mine[:, None, :] == slot, 1.0, 0.0))
    return picks


def rows_kernel(experts, blocks, me, at, routes_t, gain, conv, *refs):
    pieces, refs = refs[:blocks], refs[blocks:]
    mixed_out, refs = refs[:blocks], refs[blocks:]
    send, (normed_out, mixed, sent) = refs[:-3], refs[-3:]
    shards, _, per, rows = conv.shape
    chans = shards * per
    width = chans * blocks
    square = jnp.zeros((rows, 1), f32)
    for o in range(blocks):
        group = me[0] ^ o
        piece = pieces[o]
        gate = piece[:rows, :].astype(f32)
        sig = piece[rows : 2 * rows, :].astype(f32)
        skip = piece[2 * rows :, :].astype(f32)
        skip = skip[0:1, :] + skip[1:2, :] + skip[2:3, :]
        y = conv[:, group, :, :].astype(f32).reshape(chans, rows).T
        value = (gate * (y + skip * sig)).astype(bf16)
        mixed[group] = value
        mixed_out[o][...] = value
        value = value.astype(f32)
        square = square + jnp.sum(value * value, axis=1, keepdims=True)
    scale = lax.rsqrt(square * (1.0 / width) + 1e-05)
    for h in range(blocks):
        lanes = slice(h * chans, (h + 1) * chans)
        normed_out[:, lanes] = (mixed[h].astype(f32) * scale * gain[:, lanes]).astype(bf16)
    first, second = slots(routes_t[...], experts)
    pick = (first + second).astype(bf16).reshape(experts * CAP, rows)
    values = jnp.dot(pick, normed_out[...], preferred_element_type=f32).astype(bf16)
    _, size, _ = sent.shape
    copies = shards * size // (experts * CAP)
    if copies == 1:
        sent[...] = values.reshape(shards, size, width)
    else:
        for p in range(shards):
            e = p // copies
            sent[p] = values[e * CAP : (e + 1) * CAP, :]
    if len(send) == 1:
        send[0][...] = sent[...]
    else:
        for o in range(shards):
            send[o][...] = sent[at[0] ^ o]


def gates_kernel(normed, router, routes, gates):
    logits = jnp.dot(
        normed[...].astype(f32),
        router[...],
        precision=lax.Precision.HIGHEST,
        preferred_element_type=f32,
    )
    expert = lax.broadcasted_iota(jnp.int32, logits.shape, 1)
    for k in range(2):
        picked = jnp.where(routes[:, k : k + 1] == expert, logits, 0.0)
        value = jnp.sum(picked, axis=1, keepdims=True)
        gates[:, k : k + 1] = jax.nn.sigmoid(value)


def expert_kernel(count, *refs):
    got, (up, down), out = refs[:count], refs[count : count + 2], refs[count + 2 :]
    width = up.shape[1]
    rows = math.prod(got[0].shape[:-1])
    x = jnp.concatenate([piece[...].reshape(rows, width) for piece in got], axis=0)
    total = jnp.zeros(x.shape, f32)
    for p in range(up.shape[0]):
        hidden = jnp.dot(x, up[p], preferred_element_type=f32)
        hidden = jax.nn.gelu(hidden, approximate=True).astype(bf16)
        total = total + jnp.dot(hidden, down[p], preferred_element_type=f32)
    total = total.astype(bf16)
    for i, piece in enumerate(out):
        piece[...] = total[i * rows : (i + 1) * rows].reshape(piece.shape)


def run_experts(got, w_up, w_down, owned, group):
    width = got[0].shape[-1]
    if got[0].ndim == 2:
        slot = pl.BlockSpec((CAP, width), lambda e: (e, 0))
    else:
        slot = pl.BlockSpec((got[0].shape[0], CAP, width), lambda e: (0, e, 0))
    return pl.pallas_call(
        functools.partial(expert_kernel, len(got)),
        grid=(owned,),
        out_shape=[jax.ShapeDtypeStruct(x.shape, x.dtype) for x in got],
        in_specs=[slot] * len(got)
        + [
            pl.BlockSpec((group,) + w_up.shape[1:], lambda e: (e, 0, 0)),
            pl.BlockSpec((group,) + w_down.shape[1:], lambda e: (e, 0, 0)),
        ],
        out_specs=[slot] * len(got),
        compiler_params=params(),
        name="experts",
    )(*got, w_up, w_down)


def combine_kernel(experts, blocks, shards, me, at, routes_t, gates, *refs):
    back, out, home = refs[: -blocks - 1], refs[-blocks - 1 : -1], refs[-1]
    _, size, width = home.shape
    rows = routes_t.shape[1]
    chans = width // blocks
    copies = shards * size // (experts * CAP)
    if len(back) == 1:
        home[...] = back[0][...]
    else:
        for o in range(shards):
            home[at[0] ^ o] = back[o][...]
    picks = slots(routes_t[...], experts)
    total = jnp.zeros((rows, width), f32)
    for k in range(2):
        pick = picks[k].astype(bf16).reshape(experts * CAP, rows)
        for c in range(copies):
            if copies == 1:
                values = home[...].reshape(experts * CAP, width)
            else:
                values = jnp.concatenate([home[e * copies + c] for e in range(experts)], axis=0)
            chosen = lax.dot_general(
                pick, values, (((0,), (0,)), ((), ())), preferred_element_type=f32
            )
            total = total + gates[:, k : k + 1] * chosen
    total = total.astype(bf16)
    parts = [total[:, h * chans : (h + 1) * chans] for h in range(blocks)]
    for o in range(blocks):
        value = parts[0]
        for h in range(1, blocks):
            value = jnp.where((me[0] ^ o) == h, parts[h], value)
        out[o][...] = value


def place_kernel(me, *refs):
    pieces, out = refs[:-1], refs[-1]
    rows = pieces[0].shape[0]
    for o, piece in enumerate(pieces):
        start = pl.multiple_of((me[0] ^ o) * rows, rows)
        out[pl.ds(start, rows), :] = piece[...]


def swap(pieces, axis, offsets, total):
    return [
        piece if o == 0 else lax.ppermute(piece, axis, [(i, i ^ o) for i in range(total)])
        for o, piece in zip(offsets, pieces)
    ]


def spread_out(block, axis):
    return lax.all_to_all(block, axis, split_axis=0, concat_axis=0, tiled=True)


def body(signal, gate_v, taps, skip, norm_gain, router, w_up, w_down, routes):
    tok, chans = signal.shape
    shards, blocks = lax.axis_size("ctx"), lax.axis_size("ch")
    per, rows, width = chans // shards, tok // blocks, chans * blocks
    experts = router.shape[1]
    parts = w_up.shape[0]
    owned = max(1, parts // 2)
    group = min(parts, 2)
    size = owned * CAP
    direct = 4 <= shards <= 8
    me = lax.axis_index("ch").astype(jnp.int32).reshape(1)
    at = lax.axis_index("ctx").astype(jnp.int32).reshape(1)
    shape = jax.ShapeDtypeStruct
    around = list(range(blocks))

    spread, *pieces = call(
        functools.partial(prep_kernel, shards, blocks),
        [shape((shards, 2 * per, tok), bf16)] + [shape((2 * rows + SKIP_ROWS, chans), bf16)] * blocks,
        [me],
        [signal, taps, gate_v, skip.reshape(1, chans)],
        [],
        "prep",
        limit=PREP_LIMIT,
    )
    turns = call(
        tables_kernel,
        [shape((shards, tok), f32)] * 2 + [shape((tok, tok), bf16)] * 2,
        [],
        [],
        [],
        "tables",
        [pltpu.VMEM((tok, tok), f32)] * 2,
    )
    got = spread_out(spread, "ctx")
    pieces = swap(pieces, "ch", around, blocks)
    got, pieces = lax.optimization_barrier((got, pieces))
    conv = call(
        functools.partial(conv_kernel, blocks),
        shape((shards, blocks, per, rows), bf16),
        [],
        [],
        [got, *turns],
        "conv",
        [pltpu.VMEM((2 * shards * per, tok), bf16)] * 2 + [pltpu.VMEM((shards * per, tok), f32)] * 2,
    )
    conv = spread_out(conv.reshape(shards * blocks, per, rows), ("ctx", "ch"))
    conv = conv.reshape(shards, blocks, per, rows)
    routes_t = routes.T
    if direct:
        send_shape = [shape((size, width), bf16)] * shards
    else:
        send_shape = [shape((shards, size, width), bf16)]
    mixed_and_send = call(
        functools.partial(rows_kernel, experts, blocks),
        [shape((rows, chans), bf16)] * blocks + send_shape + [shape((rows, width), bf16)],
        [me, at],
        [],
        [routes_t, norm_gain.reshape(1, width), conv, *pieces],
        "rows",
        [pltpu.VMEM((blocks, rows, chans), bf16), pltpu.VMEM((shards, size, width), bf16)],
    )
    mixed, send, normed = mixed_and_send[:blocks], mixed_and_send[blocks:-1], mixed_and_send[-1]
    gates = call(gates_kernel, shape((rows, 2), f32), [], [], [normed, router, routes], "gates")
    if direct:
        half = shards // 2
        split = half + half // 2
        early = [0, *range(half, split), *range(1, half)]
        late = list(range(split, shards))
        there = swap([send[o] for o in early], "ctx", early, shards)
        there_late = swap([send[o] for o in late], "ctx", late, shards)
        mixed = swap(mixed, "ch", around, blocks)
        result = run_experts(there, w_up, w_down, owned, group)
        home = dict(zip(early, swap(result, "ctx", early, shards)))
        there_late, mixed = lax.optimization_barrier((there_late, mixed))
        result = run_experts(there_late, w_up, w_down, owned, group)
        home.update(zip(late, swap(result, "ctx", late, shards)))
        back = [home[o] for o in range(shards)]
    else:
        there = spread_out(send[0], "ctx")
        mixed = swap(mixed, "ch", around, blocks)
        (result,) = run_experts([there], w_up, w_down, owned, group)
        back = [spread_out(result, "ctx")]
    mixed = call(place_kernel, shape((tok, chans), bf16), [me], [], mixed, "place")
    moe = call(
        functools.partial(combine_kernel, experts, blocks, shards),
        [shape((rows, chans), bf16)] * blocks,
        [me, at],
        [],
        [routes_t, gates, *back],
        "combine",
        [pltpu.VMEM((shards, size, width), bf16)],
    )
    moe = swap(moe, "ch", around, blocks)
    moe_out = call(place_kernel, shape((tok, chans), bf16), [me], [], moe, "place")
    return (mixed, moe_out)


def solution(mesh):
    in_specs = (
        P("ctx", "ch"),
        P("ctx", "ch"),
        P("ctx", "ch"),
        P("ch"),
        P(),
        P(),
        P("ctx", None, None),
        P("ctx", None, None),
        P(("ctx", "ch"), None),
    )
    out_specs = (P("ctx", "ch"), P("ctx", "ch"))
    return jax.shard_map(body, mesh=mesh, in_specs=in_specs, out_specs=out_specs, check_vma=False)
```

```python
import functools
import math

import jax
import jax.numpy as jnp
from jax import lax
from jax.experimental import pallas as pl
from jax.experimental.pallas import tpu as pltpu
from jax.sharding import PartitionSpec as P

CAP = 16
VMEM_LIMIT = 16 * 1024 * 1024
FULL_LIMIT = 62 * 1024 * 1024

f32 = jnp.float32
bf16 = jnp.bfloat16


def params(limit=VMEM_LIMIT):
    return pltpu.CompilerParams(vmem_limit_bytes=limit)


def call(kernel, out_shape, scalars, far, operands, name, scratch=(), limit=VMEM_LIMIT, cost=None):
    vmem = pl.BlockSpec(memory_space=pltpu.VMEM)
    smem = pl.BlockSpec(memory_space=pltpu.SMEM)
    hbm = pl.BlockSpec(memory_space=pltpu.HBM)
    if far:
        held = [pltpu.VMEM(x.shape, x.dtype) for x in far]
        scratch = [*scratch, *held, pltpu.SemaphoreType.DMA((len(far),))]
    return pl.pallas_call(
        kernel,
        out_shape=out_shape,
        in_specs=[smem] * len(scalars) + [hbm] * len(far) + [vmem] * len(operands),
        out_specs=jax.tree.map(lambda _: vmem, out_shape),
        scratch_shapes=scratch,
        compiler_params=params(limit),
        cost_estimate=cost,
        name=name,
    )(*scalars, *far, *operands)


def fetch(far, held, sems):
    copies = [pltpu.make_async_copy(a, b, sems.at[i]) for i, (a, b) in enumerate(zip(far, held))]
    for copy in copies:
        copy.start()
    return copies


def cmul(a, w):
    re, im = a
    wr, wi = w.real, w.imag
    if abs(wi) < 1e-12:
        return (re, im) if wr > 0 else (-re, -im)
    if abs(wr) < 1e-12:
        return (-im, re) if wi > 0 else (im, -re)
    return (re * wr - im * wi, re * wi + im * wr)


def fft(values, sign):
    count = len(values)
    if count == 1:
        return values
    even, odd = fft(values[::2], sign), fft(values[1::2], sign)
    low, high = [], []
    for k in range(count // 2):
        angle = sign * 2.0 * math.pi * k / count
        tr, ti = cmul(odd[k], complex(math.cos(angle), math.sin(angle)))
        er, ei = even[k]
        low.append((er + tr, ei + ti))
        high.append((er - tr, ei - ti))
    return low + high


def tables_kernel(turn_cos, turn_sin, cos, sin, wide_cos, wide_sin):
    shards, length = turn_cos.shape
    shape = (shards, length)
    shard = lax.broadcasted_iota(jnp.int32, shape, 0).astype(f32) + 0.25
    lane = lax.broadcasted_iota(jnp.int32, shape, 1).astype(f32)
    angle = shard * lane * (2.0 * math.pi / (shards * length))
    turn_cos[...] = jnp.cos(angle)
    turn_sin[...] = jnp.sin(angle)
    row = lax.broadcasted_iota(jnp.int32, (8, length), 0)
    lane = lax.broadcasted_iota(jnp.int32, (8, length), 1)
    angle = ((row * lane) & (length - 1)).astype(f32) * (2.0 * math.pi / length)
    wide_cos[0:8, :] = jnp.cos(angle)
    wide_sin[0:8, :] = jnp.sin(angle)
    angle = ((lane << (row + 3)) & (length - 1)).astype(f32) * (2.0 * math.pi / length)
    step_cos, step_sin = jnp.cos(angle), jnp.sin(angle)
    count = 8
    for level in range((length // 8).bit_length() - 1):
        c, s = step_cos[level : level + 1, :], step_sin[level : level + 1, :]
        have_cos, have_sin = wide_cos[0:count, :], wide_sin[0:count, :]
        wide_cos[count : 2 * count, :] = have_cos * c - have_sin * s
        wide_sin[count : 2 * count, :] = have_sin * c + have_cos * s
        count = 2 * count
    cos[...] = wide_cos[...].astype(bf16)
    sin[...] = wide_sin[...].astype(bf16)


def prep_kernel(groups, at, *refs):
    far, refs = refs[:2], refs[2:]
    skip, spread, sig, taps, sems = refs
    copies = fetch(far, (sig, taps), sems)
    tok, chans = sig.shape
    per = chans // groups
    copies[0].wait()
    sig_t = sig[...].astype(f32).T.astype(bf16)
    for g in range(groups):
        spread[g, :per, :] = sig_t[g * per : (g + 1) * per, :]
    copies[1].wait()
    taps[0:1, :] = taps[0:1, :] + jnp.where(at[0] == 0, skip[...], 0.0)
    tap_t = taps[...].T.astype(bf16)
    for g in range(groups):
        spread[g, per:, :] = tap_t[g * per : (g + 1) * per, :]


def split_kernel(me, whole, *refs):
    pieces, sems = refs[:-1], refs[-1]
    rows = pieces[0].shape[0]
    copies = []
    for o, piece in enumerate(pieces):
        start = pl.multiple_of((me[0] ^ o) * rows, rows)
        copies.append(pltpu.make_async_copy(whole.at[pl.ds(start, rows), :], piece, sems.at[o]))
    for copy in copies:
        copy.start()
    for copy in copies:
        copy.wait()


def conv_kernel(blocks, got, turn_cos, turn_sin, cos, sin, out, are, aim, pre, pim):
    shards, twice, tok = got.shape
    per = twice // 2
    rows = tok // blocks
    step = min(per, 16)
    total = shards * tok
    half = shards * per
    twist = [
        complex(math.cos(0.5 * math.pi * j / shards), math.sin(0.5 * math.pi * j / shards))
        for j in range(shards)
    ]
    for which in range(2):
        for r in range(0, per, step):
            for b in range(blocks):
                lanes = slice(b * rows, (b + 1) * rows)
                values = []
                for j in range(shards):
                    x = got[j, which * per + r : which * per + r + step, lanes].astype(f32)
                    values.append((x * twist[j].real, x * -twist[j].imag))
                for k, (re, im) in enumerate(fft(values, -1.0)):
                    c, s = turn_cos[k : k + 1, lanes], turn_sin[k : k + 1, lanes]
                    at = which * half + k * per + r
                    are[at : at + step, lanes] = (re * c + im * s).astype(bf16)
                    aim[at : at + step, lanes] = (im * c - re * s).astype(bf16)

    def dot(a, b):
        return jnp.dot(a, b, preferred_element_type=f32)

    xr = dot(are[...], cos[...]) + dot(aim[...], sin[...])
    xi = dot(aim[...], cos[...]) - dot(are[...], sin[...])
    sr, hr, si, hi = xr[:half], xr[half:], xi[:half], xi[half:]
    prod_re = (sr * hr - si * hi).astype(bf16)
    prod_im = (sr * hi + si * hr).astype(bf16)
    pre[...] = dot(prod_re, cos[...]) - dot(prod_im, sin[...])
    pim[...] = dot(prod_im, cos[...]) + dot(prod_re, sin[...])
    for r in range(0, per, step):
        for b in range(blocks):
            lanes = slice(b * rows, (b + 1) * rows)
            values = []
            for k in range(shards):
                c, s = turn_cos[k : k + 1, lanes], turn_sin[k : k + 1, lanes]
                at = k * per + r
                re, im = pre[at : at + step, lanes], pim[at : at + step, lanes]
                values.append((re * c - im * s, im * c + re * s))
            for j, (re, im) in enumerate(fft(values, 1.0)):
                y = (re * twist[j].real - im * twist[j].imag) * (1.0 / total)
                out[j, b, r : r + step, :] = y.astype(bf16)


def slots(routes_t, experts):
    rows = routes_t.shape[1]
    expert = lax.broadcasted_iota(jnp.int32, (experts, rows), 0)
    named = [routes_t[k : k + 1, :] == expert for k in range(2)]
    either = jnp.where(named[0] | named[1], 1.0, 0.0).astype(bf16)
    before = lax.broadcasted_iota(jnp.int32, (rows, rows), 0)
    after = lax.broadcasted_iota(jnp.int32, (rows, rows), 1)
    ahead = jnp.where(before < after, 1.0, 0.0).astype(bf16)
    rank = jnp.dot(either, ahead, preferred_element_type=f32).astype(jnp.int32)
    slot = lax.broadcasted_iota(jnp.int32, (experts, CAP, rows), 1)
    picks = []
    for k in range(2):
        mine = jnp.where(named[k], rank, -1)
        picks.append(jnp.where(mine[:, None, :] == slot, 1.0, 0.0))
    return picks


def rows_kernel(experts, blocks, me, at, routes_t, gain, conv, *refs):
    pieces, refs = refs[:blocks], refs[blocks:]
    mixed_out, refs = refs[:blocks], refs[blocks:]
    send, (normed_out, mixed, sent) = refs[:-3], refs[-3:]
    shards, _, per, rows = conv.shape
    chans = shards * per
    width = chans * blocks
    square = jnp.zeros((rows, 1), f32)
    for o in range(blocks):
        group = me[0] ^ o
        y = conv[:, group, :, :].astype(f32).reshape(chans, rows).T
        value = (pieces[o][...].astype(f32) * y).astype(bf16)
        mixed[group] = value
        mixed_out[o][...] = value
        value = value.astype(f32)
        square = square + jnp.sum(value * value, axis=1, keepdims=True)
    scale = lax.rsqrt(square * (1.0 / width) + 1e-05)
    for h in range(blocks):
        lanes = slice(h * chans, (h + 1) * chans)
        normed_out[:, lanes] = (mixed[h].astype(f32) * scale * gain[:, lanes]).astype(bf16)
    first, second = slots(routes_t[...], experts)
    pick = (first + second).astype(bf16).reshape(experts * CAP, rows)
    values = jnp.dot(pick, normed_out[...], preferred_element_type=f32).astype(bf16)
    _, size, _ = sent.shape
    copies = shards * size // (experts * CAP)
    if copies == 1:
        sent[...] = values.reshape(shards, size, width)
    else:
        for p in range(shards):
            e = p // copies
            sent[p] = values[e * CAP : (e + 1) * CAP, :]
    if len(send) == 1:
        send[0][...] = sent[...]
    else:
        for o in range(shards):
            send[o][...] = sent[at[0] ^ o]


def gates_kernel(normed, router, routes, gates):
    logits = jnp.dot(
        normed[...].astype(f32),
        router[...],
        precision=lax.Precision.HIGHEST,
        preferred_element_type=f32,
    )
    expert = lax.broadcasted_iota(jnp.int32, logits.shape, 1)
    for k in range(2):
        picked = jnp.where(routes[:, k : k + 1] == expert, logits, 0.0)
        value = jnp.sum(picked, axis=1, keepdims=True)
        gates[:, k : k + 1] = jax.nn.sigmoid(value)


def expert_kernel(count, owned, up, down, *refs):
    got, out, token, x = refs[:count], refs[-2 - count : -2], refs[-2], refs[-1]
    group = up.shape[0] // owned
    width = up.shape[1]
    for e in range(owned):
        pieces = []
        for piece in got:
            if len(piece.shape) == 2:
                pieces.append(piece[e * CAP : (e + 1) * CAP, :])
            else:
                slots = piece[:, e * CAP : (e + 1) * CAP, :]
                pieces.append(slots.reshape(piece.shape[0] * CAP, width))
        x[...] = jnp.concatenate(pieces, axis=0)
        total = jnp.zeros(x.shape, f32)
        for p in range(e * group, (e + 1) * group):
            hidden = jnp.dot(x[...], up[p], preferred_element_type=f32)
            hidden = jax.nn.gelu(hidden, approximate=True).astype(bf16)
            total = total + jnp.dot(hidden, down[p], preferred_element_type=f32)
        total = total.astype(bf16)
        rows = total.shape[0] // count
        for i, piece in enumerate(out):
            part = total[i * rows : (i + 1) * rows]
            if len(piece.shape) == 2:
                piece[e * CAP : (e + 1) * CAP, :] = part
            else:
                piece[:, e * CAP : (e + 1) * CAP, :] = part.reshape(piece.shape[0], CAP, width)
    token[...] = jnp.zeros(token.shape, f32)


def run_experts(got, w_up, w_down, owned, after):
    width = got[0].shape[-1]
    slots = sum(math.prod(x.shape[:-1]) for x in got) // owned
    vmem = pl.BlockSpec(memory_space=pltpu.VMEM)
    *result, token = pl.pallas_call(
        functools.partial(expert_kernel, len(got), owned),
        out_shape=[jax.ShapeDtypeStruct(x.shape, x.dtype) for x in got]
        + [jax.ShapeDtypeStruct((8, 128), f32)],
        in_specs=[vmem] * (2 + len(got) + len(after)),
        out_specs=[vmem] * (len(got) + 1),
        scratch_shapes=[pltpu.VMEM((slots, width), bf16)],
        compiler_params=params(),
        cost_estimate=pl.CostEstimate(flops=1, bytes_accessed=1, transcendentals=0),
        name="experts",
    )(w_up, w_down, *got, *after)
    return result, [token]


def combine_kernel(experts, blocks, shards, me, at, routes_t, gates, *refs):
    back, out, home = refs[: -blocks - 1], refs[-blocks - 1 : -1], refs[-1]
    _, size, width = home.shape
    rows = routes_t.shape[1]
    chans = width // blocks
    copies = shards * size // (experts * CAP)
    if len(back) == 1:
        home[...] = back[0][...]
    else:
        for o in range(shards):
            home[at[0] ^ o] = back[o][...]
    picks = slots(routes_t[...], experts)
    total = jnp.zeros((rows, width), f32)
    for k in range(2):
        pick = picks[k].astype(bf16).reshape(experts * CAP, rows)
        for c in range(copies):
            if copies == 1:
                values = home[...].reshape(experts * CAP, width)
            else:
                values = jnp.concatenate([home[e * copies + c] for e in range(experts)], axis=0)
            chosen = lax.dot_general(
                pick, values, (((0,), (0,)), ((), ())), preferred_element_type=f32
            )
            total = total + gates[:, k : k + 1] * chosen
    total = total.astype(bf16)
    parts = [total[:, h * chans : (h + 1) * chans] for h in range(blocks)]
    for o in range(blocks):
        value = parts[0]
        for h in range(1, blocks):
            value = jnp.where((me[0] ^ o) == h, parts[h], value)
        out[o][...] = value


def place_kernel(me, *refs):
    pieces, out, sems = refs[:-2], refs[-2], refs[-1]
    rows = pieces[0].shape[0]
    copies = []
    for o, piece in enumerate(pieces):
        start = pl.multiple_of((me[0] ^ o) * rows, rows)
        copies.append(pltpu.make_async_copy(piece, out.at[pl.ds(start, rows), :], sems.at[o]))
    for copy in copies:
        copy.start()
    for copy in copies:
        copy.wait()


def split(whole, me, count):
    shape = (whole.shape[0] // count, whole.shape[1])
    return pl.pallas_call(
        split_kernel,
        out_shape=[jax.ShapeDtypeStruct(shape, whole.dtype)] * count,
        in_specs=[pl.BlockSpec(memory_space=pltpu.SMEM), pl.BlockSpec(memory_space=pltpu.HBM)],
        out_specs=[pl.BlockSpec(memory_space=pltpu.VMEM)] * count,
        scratch_shapes=[pltpu.SemaphoreType.DMA((count,))],
        compiler_params=params(),
        name="split",
    )(me, whole)


def place(pieces, me):
    count, (rows, width) = len(pieces), pieces[0].shape
    return pl.pallas_call(
        place_kernel,
        out_shape=jax.ShapeDtypeStruct((count * rows, width), pieces[0].dtype),
        in_specs=[pl.BlockSpec(memory_space=pltpu.SMEM)]
        + [pl.BlockSpec(memory_space=pltpu.VMEM)] * count,
        out_specs=pl.BlockSpec(memory_space=pltpu.HBM),
        scratch_shapes=[pltpu.SemaphoreType.DMA((count,))],
        compiler_params=params(),
        name="place",
    )(me, *pieces)


def swap(pieces, axis, offsets, total):
    return [
        piece if o == 0 else lax.ppermute(piece, axis, [(i, i ^ o) for i in range(total)])
        for o, piece in zip(offsets, pieces)
    ]


def spread_out(block, axis):
    return lax.all_to_all(block, axis, split_axis=0, concat_axis=0, tiled=True)


def body(signal, gate_v, taps, skip, norm_gain, router, w_up, w_down, routes):
    tok, chans = signal.shape
    shards, blocks = lax.axis_size("ctx"), lax.axis_size("ch")
    per, rows, width = chans // shards, tok // blocks, chans * blocks
    experts = router.shape[1]
    parts = w_up.shape[0]
    owned = max(1, parts // 2)
    size = owned * CAP
    direct = 4 <= shards <= 8
    me = lax.axis_index("ch").astype(jnp.int32).reshape(1)
    at = lax.axis_index("ctx").astype(jnp.int32).reshape(1)
    shape = jax.ShapeDtypeStruct
    around = list(range(blocks))

    spread = call(
        functools.partial(prep_kernel, shards),
        shape((shards, 2 * per, tok), bf16),
        [at],
        [signal, taps],
        [skip.reshape(1, chans)],
        "prep",
        limit=FULL_LIMIT,
    )
    pieces = split(gate_v, me, blocks)
    turns = call(
        tables_kernel,
        [shape((shards, tok), f32)] * 2 + [shape((tok, tok), bf16)] * 2,
        [],
        [],
        [],
        "tables",
        [pltpu.VMEM((tok, tok), f32)] * 2,
    )
    got = spread_out(spread, "ctx")
    own, *pieces = swap(pieces, "ch", around, blocks)
    got, pieces = lax.optimization_barrier((got, pieces))
    pieces = [own, *pieces]
    conv = call(
        functools.partial(conv_kernel, blocks),
        shape((shards, blocks, per, rows), bf16),
        [],
        [],
        [got, *turns],
        "conv",
        [pltpu.VMEM((2 * shards * per, tok), bf16)] * 2 + [pltpu.VMEM((shards * per, tok), f32)] * 2,
    )
    conv = spread_out(conv.reshape(shards * blocks, per, rows), ("ctx", "ch"))
    conv = conv.reshape(shards, blocks, per, rows)
    routes_t = routes.T
    if direct:
        send_shape = [shape((size, width), bf16)] * shards
    else:
        send_shape = [shape((shards, size, width), bf16)]
    mixed_and_send = call(
        functools.partial(rows_kernel, experts, blocks),
        [shape((rows, chans), bf16)] * blocks + send_shape + [shape((rows, width), bf16)],
        [me, at],
        [],
        [routes_t, norm_gain.reshape(1, width), conv, *pieces],
        "rows",
        [pltpu.VMEM((blocks, rows, chans), bf16), pltpu.VMEM((shards, size, width), bf16)],
    )
    mixed, send, normed = mixed_and_send[:blocks], mixed_and_send[blocks:-1], mixed_and_send[-1]
    gates = call(gates_kernel, shape((rows, 2), f32), [], [], [normed, router, routes], "gates")
    if direct:
        (own,), done = run_experts(send[:1], w_up, w_down, owned, [])
        home = {0: own}
        half = shards // 2
        cut = half + half // 2
        groups = [[*range(half, cut), *range(1, half)], list(range(cut, shards))]
        there = [swap([send[o] for o in group], "ctx", group, shards) for group in groups]
        for i, group in enumerate(groups):
            result, done = run_experts(there[i], w_up, w_down, owned, done)
            home.update(zip(group, swap(result, "ctx", group, shards)))
        back = [home[o] for o in range(shards)]
        mixed = swap(mixed, "ch", around, blocks)
    else:
        there = spread_out(send[0], "ctx")
        mixed = swap(mixed, "ch", around, blocks)
        (result,), _ = run_experts([there], w_up, w_down, owned, [])
        back = [spread_out(result, "ctx")]
    mixed = place(mixed, me)
    moe = call(
        functools.partial(combine_kernel, experts, blocks, shards),
        [shape((rows, chans), bf16)] * blocks,
        [me, at],
        [],
        [routes_t, gates, *back],
        "combine",
        [pltpu.VMEM((shards, size, width), bf16)],
    )
    moe = swap(moe, "ch", around, blocks)
    return (mixed, place(moe, me))


def solution(mesh):
    in_specs = (
        P("ctx", "ch"),
        P("ctx", "ch"),
        P("ctx", "ch"),
        P("ch"),
        P(),
        P(),
        P("ctx", None, None),
        P("ctx", None, None),
        P(("ctx", "ch"), None),
    )
    out_specs = (P("ctx", "ch"), P("ctx", "ch"))
    return jax.shard_map(body, mesh=mesh, in_specs=in_specs, out_specs=out_specs, check_vma=False)
```

```python
import functools
import math

import jax
import jax.numpy as jnp
from jax import lax
from jax.experimental import pallas as pl
from jax.experimental.pallas import tpu as pltpu
from jax.sharding import PartitionSpec as P

CAP = 16
LANES = 128
VMEM_LIMIT = 16 * 1024 * 1024
FULL_LIMIT = 62 * 1024 * 1024

f32 = jnp.float32
bf16 = jnp.bfloat16


def params(limit=VMEM_LIMIT):
    return pltpu.CompilerParams(vmem_limit_bytes=limit)


def call(kernel, out_shape, scalars, operands, name, scratch=()):
    vmem = pl.BlockSpec(memory_space=pltpu.VMEM)
    smem = pl.BlockSpec(memory_space=pltpu.SMEM)
    return pl.pallas_call(
        kernel,
        out_shape=out_shape,
        in_specs=[smem] * len(scalars) + [vmem] * len(operands),
        out_specs=jax.tree.map(lambda _: vmem, out_shape),
        scratch_shapes=scratch,
        compiler_params=params(),
        name=name,
    )(*scalars, *operands)


def cmul(a, w):
    re, im = a
    wr, wi = w.real, w.imag
    if abs(wi) < 1e-12:
        return (re, im) if wr > 0 else (-re, -im)
    if abs(wr) < 1e-12:
        return (-im, re) if wi > 0 else (im, -re)
    return (re * wr - im * wi, re * wi + im * wr)


def fft(values, sign):
    count = len(values)
    if count == 1:
        return values
    even, odd = fft(values[::2], sign), fft(values[1::2], sign)
    low, high = [], []
    for k in range(count // 2):
        angle = sign * 2.0 * math.pi * k / count
        tr, ti = cmul(odd[k], complex(math.cos(angle), math.sin(angle)))
        er, ei = even[k]
        low.append((er + tr, ei + ti))
        high.append((er - tr, ei - ti))
    return low + high


def tables_kernel(turn_cos, turn_sin, cos, sin, wide_cos, wide_sin):
    shards, length = turn_cos.shape
    shape = (shards, length)
    shard = lax.broadcasted_iota(jnp.int32, shape, 0).astype(f32) + 0.25
    lane = lax.broadcasted_iota(jnp.int32, shape, 1).astype(f32)
    angle = shard * lane * (2.0 * math.pi / (shards * length))
    turn_cos[...] = jnp.cos(angle)
    turn_sin[...] = jnp.sin(angle)
    row = lax.broadcasted_iota(jnp.int32, (8, length), 0)
    lane = lax.broadcasted_iota(jnp.int32, (8, length), 1)
    angle = ((row * lane) & (length - 1)).astype(f32) * (2.0 * math.pi / length)
    wide_cos[0:8, :] = jnp.cos(angle)
    wide_sin[0:8, :] = jnp.sin(angle)
    angle = ((lane << (row + 3)) & (length - 1)).astype(f32) * (2.0 * math.pi / length)
    step_cos, step_sin = jnp.cos(angle), jnp.sin(angle)
    count = 8
    for level in range((length // 8).bit_length() - 1):
        c, s = step_cos[level : level + 1, :], step_sin[level : level + 1, :]
        have_cos, have_sin = wide_cos[0:count, :], wide_sin[0:count, :]
        wide_cos[count : 2 * count, :] = have_cos * c - have_sin * s
        wide_sin[count : 2 * count, :] = have_sin * c + have_cos * s
        count = 2 * count
    cos[...] = wide_cos[...].astype(bf16)
    sin[...] = wide_sin[...].astype(bf16)


def prep_kernel(groups, at, far_sig, far_taps, far_skip, spread, sig, taps, skip, stage, arrive, leave):
    tok, chans = sig.shape
    per = chans // groups
    wide = LANES if chans % LANES == 0 and LANES % per == 0 else chans
    count = chans // wide
    some = groups // count
    coming = []
    early = pltpu.make_async_copy(far_skip, skip, arrive.at[2 * count])
    early.start()
    for i in range(count):
        lanes = pl.ds(i * wide, wide)
        for k, (far, held) in enumerate(((far_sig, sig), (far_taps, taps))):
            copy = pltpu.make_async_copy(
                far.at[:, lanes], held.at[:, lanes], arrive.at[2 * i + k]
            )
            copy.start()
            coming.append(copy)
    going = []
    for i in range(count):
        lanes = slice(i * wide, (i + 1) * wide)
        coming[2 * i].wait()
        sig_t = sig[:, lanes].astype(f32).T.astype(bf16)
        for g in range(some):
            stage[i * some + g, :per, :] = sig_t[g * per : (g + 1) * per, :]
        coming[2 * i + 1].wait()
        if i == 0:
            early.wait()
        taps[0:1, lanes] = taps[0:1, lanes] + jnp.where(at[0] == 0, skip[:, lanes], 0.0)
        tap_t = taps[:, lanes].T.astype(bf16)
        for g in range(some):
            stage[i * some + g, per:, :] = tap_t[g * per : (g + 1) * per, :]
        bundle = pl.ds(i * some, some)
        copy = pltpu.make_async_copy(stage.at[bundle], spread.at[bundle], leave.at[i])
        copy.start()
        going.append(copy)
    for copy in going:
        copy.wait()


def split_kernel(me, whole, *refs):
    pieces, sems = refs[:-1], refs[-1]
    rows = pieces[0].shape[0]
    copies = []
    for o, piece in enumerate(pieces):
        start = pl.multiple_of((me[0] ^ o) * rows, rows)
        copies.append(pltpu.make_async_copy(whole.at[pl.ds(start, rows), :], piece, sems.at[o]))
    for copy in copies:
        copy.start()
    for copy in copies:
        copy.wait()


def conv_kernel(blocks, got, turn_cos, turn_sin, cos, sin, out, are, aim, pre, pim):
    shards, twice, tok = got.shape
    per = twice // 2
    rows = tok // blocks
    step = min(per, 16)
    total = shards * tok
    half = shards * per
    twist = [
        complex(math.cos(0.5 * math.pi * j / shards), math.sin(0.5 * math.pi * j / shards))
        for j in range(shards)
    ]
    for which in range(2):
        for r in range(0, per, step):
            for b in range(blocks):
                lanes = slice(b * rows, (b + 1) * rows)
                values = []
                for j in range(shards):
                    x = got[j, which * per + r : which * per + r + step, lanes].astype(f32)
                    values.append((x * twist[j].real, x * -twist[j].imag))
                for k, (re, im) in enumerate(fft(values, -1.0)):
                    c, s = turn_cos[k : k + 1, lanes], turn_sin[k : k + 1, lanes]
                    at = which * half + k * per + r
                    are[at : at + step, lanes] = (re * c + im * s).astype(bf16)
                    aim[at : at + step, lanes] = (im * c - re * s).astype(bf16)

    def dot(a, b):
        return jnp.dot(a, b, preferred_element_type=f32)

    xr = dot(are[...], cos[...]) + dot(aim[...], sin[...])
    xi = dot(aim[...], cos[...]) - dot(are[...], sin[...])
    sr, hr, si, hi = xr[:half], xr[half:], xi[:half], xi[half:]
    prod_re = (sr * hr - si * hi).astype(bf16)
    prod_im = (sr * hi + si * hr).astype(bf16)
    pre[...] = dot(prod_re, cos[...]) - dot(prod_im, sin[...])
    pim[...] = dot(prod_im, cos[...]) + dot(prod_re, sin[...])
    for r in range(0, per, step):
        for b in range(blocks):
            lanes = slice(b * rows, (b + 1) * rows)
            values = []
            for k in range(shards):
                c, s = turn_cos[k : k + 1, lanes], turn_sin[k : k + 1, lanes]
                at = k * per + r
                re, im = pre[at : at + step, lanes], pim[at : at + step, lanes]
                values.append((re * c - im * s, im * c + re * s))
            for j, (re, im) in enumerate(fft(values, 1.0)):
                y = (re * twist[j].real - im * twist[j].imag) * (1.0 / total)
                out[j, b, r : r + step, :] = y.astype(bf16)


def slots(routes_t, experts):
    rows = routes_t.shape[1]
    expert = lax.broadcasted_iota(jnp.int32, (experts, rows), 0)
    named = [routes_t[k : k + 1, :] == expert for k in range(2)]
    either = jnp.where(named[0] | named[1], 1.0, 0.0).astype(bf16)
    before = lax.broadcasted_iota(jnp.int32, (rows, rows), 0)
    after = lax.broadcasted_iota(jnp.int32, (rows, rows), 1)
    ahead = jnp.where(before < after, 1.0, 0.0).astype(bf16)
    rank = jnp.dot(either, ahead, preferred_element_type=f32).astype(jnp.int32)
    slot = lax.broadcasted_iota(jnp.int32, (experts, CAP, rows), 1)
    picks = []
    for k in range(2):
        mine = jnp.where(named[k], rank, -1)
        picks.append(jnp.where(mine[:, None, :] == slot, 1.0, 0.0))
    return picks


def rows_kernel(experts, blocks, me, at, routes_t, gain, conv, *refs):
    pieces, refs = refs[:blocks], refs[blocks:]
    mixed_out, refs = refs[:blocks], refs[blocks:]
    send, (normed_out, mixed, sent) = refs[:-3], refs[-3:]
    shards, _, per, rows = conv.shape
    chans = shards * per
    width = chans * blocks
    square = jnp.zeros((rows, 1), f32)
    for o in range(blocks):
        group = me[0] ^ o
        y = conv[:, group, :, :].astype(f32).reshape(chans, rows).T
        value = (pieces[o][...].astype(f32) * y).astype(bf16)
        mixed[group] = value
        mixed_out[o][...] = value
        value = value.astype(f32)
        square = square + jnp.sum(value * value, axis=1, keepdims=True)
    scale = lax.rsqrt(square * (1.0 / width) + 1e-05)
    for h in range(blocks):
        lanes = slice(h * chans, (h + 1) * chans)
        normed_out[:, lanes] = (mixed[h].astype(f32) * scale * gain[:, lanes]).astype(bf16)
    first, second = slots(routes_t[...], experts)
    pick = (first + second).astype(bf16).reshape(experts * CAP, rows)
    values = jnp.dot(pick, normed_out[...], preferred_element_type=f32).astype(bf16)
    _, size, _ = sent.shape
    copies = shards * size // (experts * CAP)
    if copies == 1:
        sent[...] = values.reshape(shards, size, width)
    else:
        for p in range(shards):
            e = p // copies
            sent[p] = values[e * CAP : (e + 1) * CAP, :]
    if len(send) == 1:
        send[0][...] = sent[...]
    else:
        for o in range(shards):
            send[o][...] = sent[at[0] ^ o]


def gates_kernel(normed, router, routes, gates):
    logits = jnp.dot(
        normed[...].astype(f32),
        router[...],
        precision=lax.Precision.HIGHEST,
        preferred_element_type=f32,
    )
    expert = lax.broadcasted_iota(jnp.int32, logits.shape, 1)
    for k in range(2):
        picked = jnp.where(routes[:, k : k + 1] == expert, logits, 0.0)
        value = jnp.sum(picked, axis=1, keepdims=True)
        gates[:, k : k + 1] = jax.nn.sigmoid(value)


def expert_kernel(count, owned, up, down, *refs):
    got, out, x = refs[:count], refs[-1 - count : -1], refs[-1]
    group = up.shape[0] // owned
    width = up.shape[1]
    for e in range(owned):
        pieces = []
        for piece in got:
            if len(piece.shape) == 2:
                pieces.append(piece[e * CAP : (e + 1) * CAP, :])
            else:
                slots = piece[:, e * CAP : (e + 1) * CAP, :]
                pieces.append(slots.reshape(piece.shape[0] * CAP, width))
        x[...] = jnp.concatenate(pieces, axis=0)
        total = jnp.zeros(x.shape, f32)
        for p in range(e * group, (e + 1) * group):
            hidden = jnp.dot(x[...], up[p], preferred_element_type=f32)
            hidden = jax.nn.gelu(hidden, approximate=True).astype(bf16)
            total = total + jnp.dot(hidden, down[p], preferred_element_type=f32)
        total = total.astype(bf16)
        rows = total.shape[0] // count
        for i, piece in enumerate(out):
            part = total[i * rows : (i + 1) * rows]
            if len(piece.shape) == 2:
                piece[e * CAP : (e + 1) * CAP, :] = part
            else:
                piece[:, e * CAP : (e + 1) * CAP, :] = part.reshape(piece.shape[0], CAP, width)


def run_experts(got, w_up, w_down, owned, after):
    width = got[0].shape[-1]
    slots = sum(math.prod(x.shape[:-1]) for x in got) // owned
    vmem = pl.BlockSpec(memory_space=pltpu.VMEM)
    return pl.pallas_call(
        functools.partial(expert_kernel, len(got), owned),
        out_shape=[jax.ShapeDtypeStruct(x.shape, x.dtype) for x in got],
        in_specs=[vmem] * (2 + len(got) + len(after)),
        out_specs=[vmem] * len(got),
        scratch_shapes=[pltpu.VMEM((slots, width), bf16)],
        compiler_params=params(),
        cost_estimate=pl.CostEstimate(flops=1, bytes_accessed=1, transcendentals=0),
        name="experts",
    )(w_up, w_down, *got, *after)


def combine_kernel(experts, blocks, shards, me, at, routes_t, gates, *refs):
    back, out, home = refs[: -blocks - 1], refs[-blocks - 1 : -1], refs[-1]
    _, size, width = home.shape
    rows = routes_t.shape[1]
    chans = width // blocks
    copies = shards * size // (experts * CAP)
    if len(back) == 1:
        home[...] = back[0][...]
    else:
        for o in range(shards):
            home[at[0] ^ o] = back[o][...]
    picks = slots(routes_t[...], experts)
    total = jnp.zeros((rows, width), f32)
    for k in range(2):
        pick = picks[k].astype(bf16).reshape(experts * CAP, rows)
        for c in range(copies):
            if copies == 1:
                values = home[...].reshape(experts * CAP, width)
            else:
                values = jnp.concatenate([home[e * copies + c] for e in range(experts)], axis=0)
            chosen = lax.dot_general(
                pick, values, (((0,), (0,)), ((), ())), preferred_element_type=f32
            )
            total = total + gates[:, k : k + 1] * chosen
    total = total.astype(bf16)
    parts = [total[:, h * chans : (h + 1) * chans] for h in range(blocks)]
    for o in range(blocks):
        value = parts[0]
        for h in range(1, blocks):
            value = jnp.where((me[0] ^ o) == h, parts[h], value)
        out[o][...] = value


def place_kernel(me, *refs):
    pieces, out, sems = refs[:-2], refs[-2], refs[-1]
    rows = pieces[0].shape[0]
    copies = []
    for o, piece in enumerate(pieces):
        start = pl.multiple_of((me[0] ^ o) * rows, rows)
        copies.append(pltpu.make_async_copy(piece, out.at[pl.ds(start, rows), :], sems.at[o]))
    for copy in copies:
        copy.start()
    for copy in copies:
        copy.wait()


def split(whole, me, count):
    shape = (whole.shape[0] // count, whole.shape[1])
    return pl.pallas_call(
        split_kernel,
        out_shape=[jax.ShapeDtypeStruct(shape, whole.dtype)] * count,
        in_specs=[pl.BlockSpec(memory_space=pltpu.SMEM), pl.BlockSpec(memory_space=pltpu.HBM)],
        out_specs=[pl.BlockSpec(memory_space=pltpu.VMEM)] * count,
        scratch_shapes=[pltpu.SemaphoreType.DMA((count,))],
        compiler_params=params(),
        name="split",
    )(me, whole)


def place(pieces, me):
    count, (rows, width) = len(pieces), pieces[0].shape
    return pl.pallas_call(
        place_kernel,
        out_shape=jax.ShapeDtypeStruct((count * rows, width), pieces[0].dtype),
        in_specs=[pl.BlockSpec(memory_space=pltpu.SMEM)]
        + [pl.BlockSpec(memory_space=pltpu.VMEM)] * count,
        out_specs=pl.BlockSpec(memory_space=pltpu.HBM),
        scratch_shapes=[pltpu.SemaphoreType.DMA((count,))],
        compiler_params=params(),
        name="place",
    )(me, *pieces)


def swap(pieces, axis, offsets, total):
    return [
        piece if o == 0 else lax.ppermute(piece, axis, [(i, i ^ o) for i in range(total)])
        for o, piece in zip(offsets, pieces)
    ]


def spread_out(block, axis):
    return lax.all_to_all(block, axis, split_axis=0, concat_axis=0, tiled=True)


def body(signal, gate_v, taps, skip, norm_gain, router, w_up, w_down, routes):
    tok, chans = signal.shape
    shards, blocks = lax.axis_size("ctx"), lax.axis_size("ch")
    per, rows, width = chans // shards, tok // blocks, chans * blocks
    experts = router.shape[1]
    parts = w_up.shape[0]
    owned = max(1, parts // 2)
    size = owned * CAP
    direct = 4 <= shards <= 8
    me = lax.axis_index("ch").astype(jnp.int32).reshape(1)
    at = lax.axis_index("ctx").astype(jnp.int32).reshape(1)
    shape = jax.ShapeDtypeStruct
    around = list(range(blocks))

    hbm = pl.BlockSpec(memory_space=pltpu.HBM)
    steps = max(1, chans // LANES)
    spread = pl.pallas_call(
        functools.partial(prep_kernel, shards),
        out_shape=shape((shards, 2 * per, tok), bf16),
        in_specs=[pl.BlockSpec(memory_space=pltpu.SMEM), hbm, hbm, hbm],
        out_specs=hbm,
        scratch_shapes=[
            pltpu.VMEM(signal.shape, signal.dtype),
            pltpu.VMEM(taps.shape, taps.dtype),
            pltpu.VMEM((1, chans), skip.dtype),
            pltpu.VMEM((shards, 2 * per, tok), bf16),
            pltpu.SemaphoreType.DMA((2 * steps + 1,)),
            pltpu.SemaphoreType.DMA((steps,)),
        ],
        compiler_params=params(FULL_LIMIT),
        name="prep",
    )(at, signal, taps, skip.reshape(1, chans))
    pieces = split(gate_v, me, blocks)
    turns = call(
        tables_kernel,
        [shape((shards, tok), f32)] * 2 + [shape((tok, tok), bf16)] * 2,
        [],
        [],
        "tables",
        [pltpu.VMEM((tok, tok), f32)] * 2,
    )
    got = spread_out(spread, "ctx")
    own, *pieces = swap(pieces, "ch", around, blocks)
    got, pieces = lax.optimization_barrier((got, pieces))
    pieces = [own, *pieces]
    conv = call(
        functools.partial(conv_kernel, blocks),
        shape((shards, blocks, per, rows), bf16),
        [],
        [got, *turns],
        "conv",
        [pltpu.VMEM((2 * shards * per, tok), bf16)] * 2 + [pltpu.VMEM((shards * per, tok), f32)] * 2,
    )
    conv = spread_out(conv.reshape(shards * blocks, per, rows), ("ctx", "ch"))
    conv = conv.reshape(shards, blocks, per, rows)
    routes_t = routes.T
    if direct:
        send_shape = [shape((size, width), bf16)] * shards
    else:
        send_shape = [shape((shards, size, width), bf16)]
    mixed_and_send = call(
        functools.partial(rows_kernel, experts, blocks),
        [shape((rows, chans), bf16)] * blocks + send_shape + [shape((rows, width), bf16)],
        [me, at],
        [routes_t, norm_gain.reshape(1, width), conv, *pieces],
        "rows",
        [pltpu.VMEM((blocks, rows, chans), bf16), pltpu.VMEM((shards, size, width), bf16)],
    )
    mixed, send, normed = mixed_and_send[:blocks], mixed_and_send[blocks:-1], mixed_and_send[-1]
    gates = call(gates_kernel, shape((rows, 2), f32), [], [normed, router, routes], "gates")
    if direct:
        done = run_experts(send[:1], w_up, w_down, owned, [])
        home = {0: done[0]}
        half = shards // 2
        cut = half + half // 2
        groups = [[*range(half, cut), *reversed(range(1, half))], list(range(cut, shards))]
        there = [swap([send[o] for o in group], "ctx", group, shards) for group in groups]
        for i, group in enumerate(groups):
            done = run_experts(there[i], w_up, w_down, owned, done[:1])
            home.update(zip(group, swap(done, "ctx", group, shards)))
        back = [home[o] for o in range(shards)]
        mixed = swap(mixed, "ch", around, blocks)
    else:
        there = spread_out(send[0], "ctx")
        mixed = swap(mixed, "ch", around, blocks)
        (result,) = run_experts([there], w_up, w_down, owned, [])
        back = [spread_out(result, "ctx")]
    mixed = place(mixed, me)
    moe = call(
        functools.partial(combine_kernel, experts, blocks, shards),
        [shape((rows, chans), bf16)] * blocks,
        [me, at],
        [routes_t, gates, *back],
        "combine",
        [pltpu.VMEM((shards, size, width), bf16)],
    )
    moe = swap(moe, "ch", around, blocks)
    return (mixed, place(moe, me))


def solution(mesh):
    in_specs = (
        P("ctx", "ch"),
        P("ctx", "ch"),
        P("ctx", "ch"),
        P("ch"),
        P(),
        P(),
        P("ctx", None, None),
        P("ctx", None, None),
        P(("ctx", "ch"), None),
    )
    out_specs = (P("ctx", "ch"), P("ctx", "ch"))
    return jax.shard_map(body, mesh=mesh, in_specs=in_specs, out_specs=out_specs, check_vma=False)
```

```python
import functools
import math

import jax
import jax.numpy as jnp
from jax import lax
from jax.experimental import pallas as pl
from jax.experimental.pallas import tpu as pltpu
from jax.sharding import PartitionSpec as P

CAP = 16
LANES = 128
VMEM_LIMIT = 16 * 1024 * 1024
FULL_LIMIT = 62 * 1024 * 1024

f32 = jnp.float32
bf16 = jnp.bfloat16


def params(limit=VMEM_LIMIT):
    return pltpu.CompilerParams(vmem_limit_bytes=limit)


def call(kernel, out_shape, scalars, operands, name, scratch=()):
    vmem = pl.BlockSpec(memory_space=pltpu.VMEM)
    smem = pl.BlockSpec(memory_space=pltpu.SMEM)
    return pl.pallas_call(
        kernel,
        out_shape=out_shape,
        in_specs=[smem] * len(scalars) + [vmem] * len(operands),
        out_specs=jax.tree.map(lambda _: vmem, out_shape),
        scratch_shapes=scratch,
        compiler_params=params(),
        name=name,
    )(*scalars, *operands)


def cmul(a, w):
    re, im = a
    wr, wi = w.real, w.imag
    if abs(wi) < 1e-12:
        return (re, im) if wr > 0 else (-re, -im)
    if abs(wr) < 1e-12:
        return (-im, re) if wi > 0 else (im, -re)
    return (re * wr - im * wi, re * wi + im * wr)


def fft(values, sign):
    count = len(values)
    if count == 1:
        return values
    even, odd = fft(values[::2], sign), fft(values[1::2], sign)
    low, high = [], []
    for k in range(count // 2):
        angle = sign * 2.0 * math.pi * k / count
        tr, ti = cmul(odd[k], complex(math.cos(angle), math.sin(angle)))
        er, ei = even[k]
        low.append((er + tr, ei + ti))
        high.append((er - tr, ei - ti))
    return low + high


def tables_kernel(turn_cos, turn_sin, cos, sin, wide_cos, wide_sin):
    shards, length = turn_cos.shape
    shape = (shards, length)
    shard = lax.broadcasted_iota(jnp.int32, shape, 0).astype(f32) + 0.25
    lane = lax.broadcasted_iota(jnp.int32, shape, 1).astype(f32)
    angle = shard * lane * (2.0 * math.pi / (shards * length))
    turn_cos[...] = jnp.cos(angle)
    turn_sin[...] = jnp.sin(angle)
    row = lax.broadcasted_iota(jnp.int32, (8, length), 0)
    lane = lax.broadcasted_iota(jnp.int32, (8, length), 1)
    angle = ((row * lane) & (length - 1)).astype(f32) * (2.0 * math.pi / length)
    wide_cos[0:8, :] = jnp.cos(angle)
    wide_sin[0:8, :] = jnp.sin(angle)
    angle = ((lane << (row + 3)) & (length - 1)).astype(f32) * (2.0 * math.pi / length)
    step_cos, step_sin = jnp.cos(angle), jnp.sin(angle)
    count = 8
    for level in range((length // 8).bit_length() - 1):
        c, s = step_cos[level : level + 1, :], step_sin[level : level + 1, :]
        have_cos, have_sin = wide_cos[0:count, :], wide_sin[0:count, :]
        wide_cos[count : 2 * count, :] = have_cos * c - have_sin * s
        wide_sin[count : 2 * count, :] = have_sin * c + have_cos * s
        count = 2 * count
    cos[...] = wide_cos[...].astype(bf16)
    sin[...] = wide_sin[...].astype(bf16)


def prep_kernel(groups, at, far_sig, far_taps, far_skip, spread, sig, taps, skip, stage, arrive, leave):
    tok, chans = sig.shape
    per = chans // groups
    wide = LANES if chans % LANES == 0 and LANES % per == 0 else chans
    count = chans // wide
    some = groups // count
    coming = []
    early = pltpu.make_async_copy(far_skip, skip, arrive.at[2 * count])
    early.start()
    for i in range(count):
        lanes = pl.ds(i * wide, wide)
        for k, (far, held) in enumerate(((far_sig, sig), (far_taps, taps))):
            copy = pltpu.make_async_copy(
                far.at[:, lanes], held.at[:, lanes], arrive.at[2 * i + k]
            )
            copy.start()
            coming.append(copy)
    going = []
    for i in range(count):
        lanes = slice(i * wide, (i + 1) * wide)
        coming[2 * i].wait()
        sig_t = sig[:, lanes].astype(f32).T.astype(bf16)
        for g in range(some):
            stage[i * some + g, :per, :] = sig_t[g * per : (g + 1) * per, :]
        coming[2 * i + 1].wait()
        if i == 0:
            early.wait()
        taps[0:1, lanes] = taps[0:1, lanes] + jnp.where(at[0] == 0, skip[:, lanes], 0.0)
        tap_t = taps[:, lanes].T.astype(bf16)
        for g in range(some):
            stage[i * some + g, per:, :] = tap_t[g * per : (g + 1) * per, :]
        bundle = pl.ds(i * some, some)
        copy = pltpu.make_async_copy(stage.at[bundle], spread.at[bundle], leave.at[i])
        copy.start()
        going.append(copy)
    for copy in going:
        copy.wait()


def split_kernel(me, whole, *refs):
    pieces, sems = refs[:-1], refs[-1]
    rows = pieces[0].shape[0]
    copies = []
    for o, piece in enumerate(pieces):
        start = pl.multiple_of((me[0] ^ o) * rows, rows)
        copies.append(pltpu.make_async_copy(whole.at[pl.ds(start, rows), :], piece, sems.at[o]))
    for copy in copies:
        copy.start()
    for copy in copies:
        copy.wait()


def conv_kernel(blocks, got, turn_cos, turn_sin, cos, sin, out, are, aim, pre, pim):
    shards, twice, tok = got.shape
    per = twice // 2
    rows = tok // blocks
    step = min(per, 16)
    total = shards * tok
    half = shards * per
    twist = [
        complex(math.cos(0.5 * math.pi * j / shards), math.sin(0.5 * math.pi * j / shards))
        for j in range(shards)
    ]
    for which in range(2):
        for r in range(0, per, step):
            for b in range(blocks):
                lanes = slice(b * rows, (b + 1) * rows)
                values = []
                for j in range(shards):
                    x = got[j, which * per + r : which * per + r + step, lanes].astype(f32)
                    values.append((x * twist[j].real, x * -twist[j].imag))
                for k, (re, im) in enumerate(fft(values, -1.0)):
                    c, s = turn_cos[k : k + 1, lanes], turn_sin[k : k + 1, lanes]
                    at = which * half + k * per + r
                    are[at : at + step, lanes] = (re * c + im * s).astype(bf16)
                    aim[at : at + step, lanes] = (im * c - re * s).astype(bf16)

    def dot(a, b):
        return jnp.dot(a, b, preferred_element_type=f32)

    xr = dot(are[...], cos[...]) + dot(aim[...], sin[...])
    xi = dot(aim[...], cos[...]) - dot(are[...], sin[...])
    sr, hr, si, hi = xr[:half], xr[half:], xi[:half], xi[half:]
    prod_re = (sr * hr - si * hi).astype(bf16)
    prod_im = (sr * hi + si * hr).astype(bf16)
    pre[...] = dot(prod_re, cos[...]) - dot(prod_im, sin[...])
    pim[...] = dot(prod_im, cos[...]) + dot(prod_re, sin[...])
    for r in range(0, per, step):
        for b in range(blocks):
            lanes = slice(b * rows, (b + 1) * rows)
            values = []
            for k in range(shards):
                c, s = turn_cos[k : k + 1, lanes], turn_sin[k : k + 1, lanes]
                at = k * per + r
                re, im = pre[at : at + step, lanes], pim[at : at + step, lanes]
                values.append((re * c - im * s, im * c + re * s))
            for j, (re, im) in enumerate(fft(values, 1.0)):
                y = (re * twist[j].real - im * twist[j].imag) * (1.0 / total)
                out[j, b, r : r + step, :] = y.astype(bf16)


def slots(routes_t, experts):
    rows = routes_t.shape[1]
    expert = lax.broadcasted_iota(jnp.int32, (experts, rows), 0)
    named = [routes_t[k : k + 1, :] == expert for k in range(2)]
    either = jnp.where(named[0] | named[1], 1.0, 0.0).astype(bf16)
    before = lax.broadcasted_iota(jnp.int32, (rows, rows), 0)
    after = lax.broadcasted_iota(jnp.int32, (rows, rows), 1)
    ahead = jnp.where(before < after, 1.0, 0.0).astype(bf16)
    rank = jnp.dot(either, ahead, preferred_element_type=f32).astype(jnp.int32)
    slot = lax.broadcasted_iota(jnp.int32, (experts, CAP, rows), 1)
    picks = []
    for k in range(2):
        mine = jnp.where(named[k], rank, -1)
        picks.append(jnp.where(mine[:, None, :] == slot, 1.0, 0.0))
    return picks


def picks_kernel(experts, routes_t, *out):
    for pick, ref in zip(slots(routes_t[...], experts), out):
        ref[...] = pick.astype(bf16).reshape(ref.shape)


def rows_kernel(experts, blocks, me, at, first, second, gain, conv, *refs):
    pieces, refs = refs[:blocks], refs[blocks:]
    mixed_out, refs = refs[:blocks], refs[blocks:]
    send, (normed_out, mixed, sent) = refs[:-3], refs[-3:]
    shards, _, per, rows = conv.shape
    chans = shards * per
    width = chans * blocks
    square = jnp.zeros((rows, 1), f32)
    for o in range(blocks):
        group = me[0] ^ o
        y = conv[:, group, :, :].astype(f32).reshape(chans, rows).T
        value = (pieces[o][...].astype(f32) * y).astype(bf16)
        mixed[group] = value
        mixed_out[o][...] = value
        value = value.astype(f32)
        square = square + jnp.sum(value * value, axis=1, keepdims=True)
    scale = lax.rsqrt(square * (1.0 / width) + 1e-05)
    for h in range(blocks):
        lanes = slice(h * chans, (h + 1) * chans)
        normed_out[:, lanes] = (mixed[h].astype(f32) * scale * gain[:, lanes]).astype(bf16)
    pick = first[...] + second[...]
    values = jnp.dot(pick, normed_out[...], preferred_element_type=f32).astype(bf16)
    _, size, _ = sent.shape
    copies = shards * size // (experts * CAP)
    if copies == 1:
        sent[...] = values.reshape(shards, size, width)
    else:
        for p in range(shards):
            e = p // copies
            sent[p] = values[e * CAP : (e + 1) * CAP, :]
    if len(send) == 1:
        send[0][...] = sent[...]
    else:
        for o in range(shards):
            send[o][...] = sent[at[0] ^ o]


def gates_kernel(normed, router, routes, gates):
    logits = jnp.dot(
        normed[...].astype(f32),
        router[...],
        precision=lax.Precision.HIGHEST,
        preferred_element_type=f32,
    )
    expert = lax.broadcasted_iota(jnp.int32, logits.shape, 1)
    for k in range(2):
        picked = jnp.where(routes[:, k : k + 1] == expert, logits, 0.0)
        value = jnp.sum(picked, axis=1, keepdims=True)
        gates[:, k : k + 1] = jax.nn.sigmoid(value)


def expert_kernel(count, owned, up, down, *refs):
    got, out, x = refs[:count], refs[-1 - count : -1], refs[-1]
    group = up.shape[0] // owned
    width = up.shape[1]
    for e in range(owned):
        pieces = []
        for piece in got:
            if len(piece.shape) == 2:
                pieces.append(piece[e * CAP : (e + 1) * CAP, :])
            else:
                slots = piece[:, e * CAP : (e + 1) * CAP, :]
                pieces.append(slots.reshape(piece.shape[0] * CAP, width))
        x[...] = jnp.concatenate(pieces, axis=0)
        total = jnp.zeros(x.shape, f32)
        for p in range(e * group, (e + 1) * group):
            hidden = jnp.dot(x[...], up[p], preferred_element_type=f32)
            hidden = jax.nn.gelu(hidden, approximate=True).astype(bf16)
            total = total + jnp.dot(hidden, down[p], preferred_element_type=f32)
        total = total.astype(bf16)
        rows = total.shape[0] // count
        for i, piece in enumerate(out):
            part = total[i * rows : (i + 1) * rows]
            if len(piece.shape) == 2:
                piece[e * CAP : (e + 1) * CAP, :] = part
            else:
                piece[:, e * CAP : (e + 1) * CAP, :] = part.reshape(piece.shape[0], CAP, width)


def run_experts(got, w_up, w_down, owned, after):
    width = got[0].shape[-1]
    slots = sum(math.prod(x.shape[:-1]) for x in got) // owned
    vmem = pl.BlockSpec(memory_space=pltpu.VMEM)
    return pl.pallas_call(
        functools.partial(expert_kernel, len(got), owned),
        out_shape=[jax.ShapeDtypeStruct(x.shape, x.dtype) for x in got],
        in_specs=[vmem] * (2 + len(got) + len(after)),
        out_specs=[vmem] * len(got),
        scratch_shapes=[pltpu.VMEM((slots, width), bf16)],
        compiler_params=params(),
        cost_estimate=pl.CostEstimate(flops=1, bytes_accessed=1, transcendentals=0),
        name="experts",
    )(w_up, w_down, *got, *after)


def combine_kernel(experts, blocks, shards, me, at, first, second, gates, *refs):
    back, out, home = refs[: -blocks - 1], refs[-blocks - 1 : -1], refs[-1]
    _, size, width = home.shape
    rows = first.shape[1]
    chans = width // blocks
    copies = shards * size // (experts * CAP)
    if len(back) == 1:
        home[...] = back[0][...]
    else:
        for o in range(shards):
            home[at[0] ^ o] = back[o][...]
    picks = (first, second)
    total = jnp.zeros((rows, width), f32)
    for k in range(2):
        pick = picks[k][...]
        for c in range(copies):
            if copies == 1:
                values = home[...].reshape(experts * CAP, width)
            else:
                values = jnp.concatenate([home[e * copies + c] for e in range(experts)], axis=0)
            chosen = lax.dot_general(
                pick, values, (((0,), (0,)), ((), ())), preferred_element_type=f32
            )
            total = total + gates[:, k : k + 1] * chosen
    total = total.astype(bf16)
    parts = [total[:, h * chans : (h + 1) * chans] for h in range(blocks)]
    for o in range(blocks):
        value = parts[0]
        for h in range(1, blocks):
            value = jnp.where((me[0] ^ o) == h, parts[h], value)
        out[o][...] = value


def place_kernel(me, *refs):
    pieces, out, sems = refs[:-2], refs[-2], refs[-1]
    rows = pieces[0].shape[0]
    copies = []
    for o, piece in enumerate(pieces):
        start = pl.multiple_of((me[0] ^ o) * rows, rows)
        copies.append(pltpu.make_async_copy(piece, out.at[pl.ds(start, rows), :], sems.at[o]))
    for copy in copies:
        copy.start()
    for copy in copies:
        copy.wait()


def split(whole, me, count):
    shape = (whole.shape[0] // count, whole.shape[1])
    return pl.pallas_call(
        split_kernel,
        out_shape=[jax.ShapeDtypeStruct(shape, whole.dtype)] * count,
        in_specs=[pl.BlockSpec(memory_space=pltpu.SMEM), pl.BlockSpec(memory_space=pltpu.HBM)],
        out_specs=[pl.BlockSpec(memory_space=pltpu.VMEM)] * count,
        scratch_shapes=[pltpu.SemaphoreType.DMA((count,))],
        compiler_params=params(),
        name="split",
    )(me, whole)


def place(pieces, me):
    count, (rows, width) = len(pieces), pieces[0].shape
    return pl.pallas_call(
        place_kernel,
        out_shape=jax.ShapeDtypeStruct((count * rows, width), pieces[0].dtype),
        in_specs=[pl.BlockSpec(memory_space=pltpu.SMEM)]
        + [pl.BlockSpec(memory_space=pltpu.VMEM)] * count,
        out_specs=pl.BlockSpec(memory_space=pltpu.HBM),
        scratch_shapes=[pltpu.SemaphoreType.DMA((count,))],
        compiler_params=params(),
        name="place",
    )(me, *pieces)


def swap(pieces, axis, offsets, total):
    return [
        piece if o == 0 else lax.ppermute(piece, axis, [(i, i ^ o) for i in range(total)])
        for o, piece in zip(offsets, pieces)
    ]


def spread_out(block, axis):
    return lax.all_to_all(block, axis, split_axis=0, concat_axis=0, tiled=True)


def body(signal, gate_v, taps, skip, norm_gain, router, w_up, w_down, routes):
    tok, chans = signal.shape
    shards, blocks = lax.axis_size("ctx"), lax.axis_size("ch")
    per, rows, width = chans // shards, tok // blocks, chans * blocks
    experts = router.shape[1]
    parts = w_up.shape[0]
    owned = max(1, parts // 2)
    size = owned * CAP
    direct = 4 <= shards <= 8
    me = lax.axis_index("ch").astype(jnp.int32).reshape(1)
    at = lax.axis_index("ctx").astype(jnp.int32).reshape(1)
    shape = jax.ShapeDtypeStruct
    around = list(range(blocks))

    hbm = pl.BlockSpec(memory_space=pltpu.HBM)
    steps = max(1, chans // LANES)
    spread = pl.pallas_call(
        functools.partial(prep_kernel, shards),
        out_shape=shape((shards, 2 * per, tok), bf16),
        in_specs=[pl.BlockSpec(memory_space=pltpu.SMEM), hbm, hbm, hbm],
        out_specs=hbm,
        scratch_shapes=[
            pltpu.VMEM(signal.shape, signal.dtype),
            pltpu.VMEM(taps.shape, taps.dtype),
            pltpu.VMEM((1, chans), skip.dtype),
            pltpu.VMEM((shards, 2 * per, tok), bf16),
            pltpu.SemaphoreType.DMA((2 * steps + 1,)),
            pltpu.SemaphoreType.DMA((steps,)),
        ],
        compiler_params=params(FULL_LIMIT),
        name="prep",
    )(at, signal, taps, skip.reshape(1, chans))
    pieces = split(gate_v, me, blocks)
    turns = call(
        tables_kernel,
        [shape((shards, tok), f32)] * 2 + [shape((tok, tok), bf16)] * 2,
        [],
        [],
        "tables",
        [pltpu.VMEM((tok, tok), f32)] * 2,
    )
    got = spread_out(spread, "ctx")
    own, *pieces = swap(pieces, "ch", around, blocks)
    picks = call(
        functools.partial(picks_kernel, experts),
        [shape((experts * CAP, rows), bf16)] * 2,
        [],
        [routes.T],
        "picks",
    )
    got, pieces, picks = lax.optimization_barrier((got, pieces, picks))
    pieces = [own, *pieces]
    conv = call(
        functools.partial(conv_kernel, blocks),
        shape((shards, blocks, per, rows), bf16),
        [],
        [got, *turns],
        "conv",
        [pltpu.VMEM((2 * shards * per, tok), bf16)] * 2 + [pltpu.VMEM((shards * per, tok), f32)] * 2,
    )
    conv = spread_out(conv.reshape(shards * blocks, per, rows), ("ctx", "ch"))
    conv = conv.reshape(shards, blocks, per, rows)
    if direct:
        send_shape = [shape((size, width), bf16)] * shards
    else:
        send_shape = [shape((shards, size, width), bf16)]
    mixed_and_send = call(
        functools.partial(rows_kernel, experts, blocks),
        [shape((rows, chans), bf16)] * blocks + send_shape + [shape((rows, width), bf16)],
        [me, at],
        [*picks, norm_gain.reshape(1, width), conv, *pieces],
        "rows",
        [pltpu.VMEM((blocks, rows, chans), bf16), pltpu.VMEM((shards, size, width), bf16)],
    )
    mixed, send, normed = mixed_and_send[:blocks], mixed_and_send[blocks:-1], mixed_and_send[-1]
    gates = call(gates_kernel, shape((rows, 2), f32), [], [normed, router, routes], "gates")
    if direct:
        done = run_experts(send[:1], w_up, w_down, owned, [])
        home = {0: done[0]}
        half = shards // 2
        cut = half + half // 2
        groups = [[*range(half, cut), *reversed(range(1, half))], list(range(cut, shards))]
        there = [swap([send[o] for o in group], "ctx", group, shards) for group in groups]
        for i, group in enumerate(groups):
            done = run_experts(there[i], w_up, w_down, owned, done[:1])
            home.update(zip(group, swap(done, "ctx", group, shards)))
        back = [home[o] for o in range(shards)]
        mixed = swap(mixed, "ch", around, blocks)
    else:
        there = spread_out(send[0], "ctx")
        mixed = swap(mixed, "ch", around, blocks)
        (result,) = run_experts([there], w_up, w_down, owned, [])
        back = [spread_out(result, "ctx")]
    mixed = place(mixed, me)
    moe = call(
        functools.partial(combine_kernel, experts, blocks, shards),
        [shape((rows, chans), bf16)] * blocks,
        [me, at],
        [*picks, gates, *back],
        "combine",
        [pltpu.VMEM((shards, size, width), bf16)],
    )
    moe = swap(moe, "ch", around, blocks)
    return (mixed, place(moe, me))


def solution(mesh):
    in_specs = (
        P("ctx", "ch"),
        P("ctx", "ch"),
        P("ctx", "ch"),
        P("ch"),
        P(),
        P(),
        P("ctx", None, None),
        P("ctx", None, None),
        P(("ctx", "ch"), None),
    )
    out_specs = (P("ctx", "ch"), P("ctx", "ch"))
    return jax.shard_map(body, mesh=mesh, in_specs=in_specs, out_specs=out_specs, check_vma=False)
```

```python
import functools
import math

import jax
import jax.numpy as jnp
from jax import lax
from jax.experimental import pallas as pl
from jax.experimental.pallas import tpu as pltpu
from jax.sharding import PartitionSpec as P

CAP = 16
LANES = 128
VMEM_LIMIT = 16 * 1024 * 1024
FULL_LIMIT = 62 * 1024 * 1024

f32 = jnp.float32
bf16 = jnp.bfloat16


def params(limit=VMEM_LIMIT):
    return pltpu.CompilerParams(vmem_limit_bytes=limit)


def call(kernel, out_shape, scalars, operands, name, scratch=()):
    vmem = pl.BlockSpec(memory_space=pltpu.VMEM)
    smem = pl.BlockSpec(memory_space=pltpu.SMEM)
    return pl.pallas_call(
        kernel,
        out_shape=out_shape,
        in_specs=[smem] * len(scalars) + [vmem] * len(operands),
        out_specs=jax.tree.map(lambda _: vmem, out_shape),
        scratch_shapes=scratch,
        compiler_params=params(),
        name=name,
    )(*scalars, *operands)


def cmul(a, w):
    re, im = a
    wr, wi = w.real, w.imag
    if abs(wi) < 1e-12:
        return (re, im) if wr > 0 else (-re, -im)
    if abs(wr) < 1e-12:
        return (-im, re) if wi > 0 else (im, -re)
    return (re * wr - im * wi, re * wi + im * wr)


def fft(values, sign):
    count = len(values)
    if count == 1:
        return values
    even, odd = fft(values[::2], sign), fft(values[1::2], sign)
    low, high = [], []
    for k in range(count // 2):
        angle = sign * 2.0 * math.pi * k / count
        tr, ti = cmul(odd[k], complex(math.cos(angle), math.sin(angle)))
        er, ei = even[k]
        low.append((er + tr, ei + ti))
        high.append((er - tr, ei - ti))
    return low + high


def tables_kernel(turn_cos, turn_sin, cos, sin, wide_cos, wide_sin):
    shards, length = turn_cos.shape
    shape = (shards, length)
    shard = lax.broadcasted_iota(jnp.int32, shape, 0).astype(f32) + 0.25
    lane = lax.broadcasted_iota(jnp.int32, shape, 1).astype(f32)
    angle = shard * lane * (2.0 * math.pi / (shards * length))
    turn_cos[...] = jnp.cos(angle)
    turn_sin[...] = jnp.sin(angle)
    row = lax.broadcasted_iota(jnp.int32, (8, length), 0)
    lane = lax.broadcasted_iota(jnp.int32, (8, length), 1)
    angle = ((row * lane) & (length - 1)).astype(f32) * (2.0 * math.pi / length)
    wide_cos[0:8, :] = jnp.cos(angle)
    wide_sin[0:8, :] = jnp.sin(angle)
    angle = ((lane << (row + 3)) & (length - 1)).astype(f32) * (2.0 * math.pi / length)
    step_cos, step_sin = jnp.cos(angle), jnp.sin(angle)
    count = 8
    for level in range((length // 8).bit_length() - 1):
        c, s = step_cos[level : level + 1, :], step_sin[level : level + 1, :]
        have_cos, have_sin = wide_cos[0:count, :], wide_sin[0:count, :]
        wide_cos[count : 2 * count, :] = have_cos * c - have_sin * s
        wide_sin[count : 2 * count, :] = have_sin * c + have_cos * s
        count = 2 * count
    cos[...] = wide_cos[...].astype(bf16)
    sin[...] = wide_sin[...].astype(bf16)


def prep_kernel(groups, at, far_sig, far_taps, far_skip, spread, sig, taps, skip, stage, arrive, leave):
    tok, chans = sig.shape
    per = chans // groups
    wide = LANES if chans % LANES == 0 and LANES % per == 0 else chans
    count = chans // wide
    some = groups // count
    coming = []
    early = pltpu.make_async_copy(far_skip, skip, arrive.at[2 * count])
    early.start()
    for i in range(count):
        lanes = pl.ds(i * wide, wide)
        for k, (far, held) in enumerate(((far_sig, sig), (far_taps, taps))):
            copy = pltpu.make_async_copy(
                far.at[:, lanes], held.at[:, lanes], arrive.at[2 * i + k]
            )
            copy.start()
            coming.append(copy)
    going = []
    for i in range(count):
        lanes = slice(i * wide, (i + 1) * wide)
        coming[2 * i].wait()
        sig_t = sig[:, lanes].astype(f32).T.astype(bf16)
        for g in range(some):
            stage[i * some + g, :per, :] = sig_t[g * per : (g + 1) * per, :]
        coming[2 * i + 1].wait()
        if i == 0:
            early.wait()
        taps[0:1, lanes] = taps[0:1, lanes] + jnp.where(at[0] == 0, skip[:, lanes], 0.0)
        tap_t = taps[:, lanes].T.astype(bf16)
        for g in range(some):
            stage[i * some + g, per:, :] = tap_t[g * per : (g + 1) * per, :]
        bundle = pl.ds(i * some, some)
        copy = pltpu.make_async_copy(stage.at[bundle], spread.at[bundle], leave.at[i])
        copy.start()
        going.append(copy)
    for copy in going:
        copy.wait()


def split_kernel(me, whole, *refs):
    pieces, sems = refs[:-1], refs[-1]
    rows = pieces[0].shape[0]
    copies = []
    for o, piece in enumerate(pieces):
        start = pl.multiple_of((me[0] ^ o) * rows, rows)
        copies.append(pltpu.make_async_copy(whole.at[pl.ds(start, rows), :], piece, sems.at[o]))
    for copy in copies:
        copy.start()
    for copy in copies:
        copy.wait()


def conv_kernel(blocks, got, turn_cos, turn_sin, cos, sin, out, are, aim, pre, pim):
    shards, twice, tok = got.shape
    per = twice // 2
    rows = tok // blocks
    step = min(per, 16)
    total = shards * tok
    half = shards * per
    twist = [
        complex(math.cos(0.5 * math.pi * j / shards), math.sin(0.5 * math.pi * j / shards))
        for j in range(shards)
    ]
    for which in range(2):
        for r in range(0, per, step):
            for b in range(blocks):
                lanes = slice(b * rows, (b + 1) * rows)
                values = []
                for j in range(shards):
                    x = got[j, which * per + r : which * per + r + step, lanes].astype(f32)
                    values.append((x * twist[j].real, x * -twist[j].imag))
                for k, (re, im) in enumerate(fft(values, -1.0)):
                    c, s = turn_cos[k : k + 1, lanes], turn_sin[k : k + 1, lanes]
                    at = which * half + k * per + r
                    are[at : at + step, lanes] = (re * c + im * s).astype(bf16)
                    aim[at : at + step, lanes] = (im * c - re * s).astype(bf16)

    def dot(a, b):
        return jnp.dot(a, b, preferred_element_type=f32)

    xr = dot(are[...], cos[...]) + dot(aim[...], sin[...])
    xi = dot(aim[...], cos[...]) - dot(are[...], sin[...])
    sr, hr, si, hi = xr[:half], xr[half:], xi[:half], xi[half:]
    prod_re = (sr * hr - si * hi).astype(bf16)
    prod_im = (sr * hi + si * hr).astype(bf16)
    pre[...] = dot(prod_re, cos[...]) - dot(prod_im, sin[...])
    pim[...] = dot(prod_im, cos[...]) + dot(prod_re, sin[...])
    for r in range(0, per, step):
        for b in range(blocks):
            lanes = slice(b * rows, (b + 1) * rows)
            values = []
            for k in range(shards):
                c, s = turn_cos[k : k + 1, lanes], turn_sin[k : k + 1, lanes]
                at = k * per + r
                re, im = pre[at : at + step, lanes], pim[at : at + step, lanes]
                values.append((re * c - im * s, im * c + re * s))
            for j, (re, im) in enumerate(fft(values, 1.0)):
                y = (re * twist[j].real - im * twist[j].imag) * (1.0 / total)
                out[j, b, r : r + step, :] = y.astype(bf16)


def slots(routes_t, experts):
    rows = routes_t.shape[1]
    expert = lax.broadcasted_iota(jnp.int32, (experts, rows), 0)
    named = [routes_t[k : k + 1, :] == expert for k in range(2)]
    either = jnp.where(named[0] | named[1], 1.0, 0.0).astype(bf16)
    before = lax.broadcasted_iota(jnp.int32, (rows, rows), 0)
    after = lax.broadcasted_iota(jnp.int32, (rows, rows), 1)
    ahead = jnp.where(before < after, 1.0, 0.0).astype(bf16)
    rank = jnp.dot(either, ahead, preferred_element_type=f32).astype(jnp.int32)
    slot = lax.broadcasted_iota(jnp.int32, (experts, CAP, rows), 1)
    picks = []
    for k in range(2):
        mine = jnp.where(named[k], rank, -1)
        picks.append(jnp.where(mine[:, None, :] == slot, 1.0, 0.0))
    return picks


def rows_kernel(experts, blocks, me, at, routes_t, gain, conv, *refs):
    pieces, refs = refs[:blocks], refs[blocks:]
    mixed_out, refs = refs[:blocks], refs[blocks:]
    send, (normed_out, mixed, sent) = refs[:-3], refs[-3:]
    shards, _, per, rows = conv.shape
    chans = shards * per
    width = chans * blocks
    square = jnp.zeros((rows, 1), f32)
    for o in range(blocks):
        group = me[0] ^ o
        y = conv[:, group, :, :].astype(f32).reshape(chans, rows).T
        value = (pieces[o][...].astype(f32) * y).astype(bf16)
        mixed[group] = value
        mixed_out[o][...] = value
        value = value.astype(f32)
        square = square + jnp.sum(value * value, axis=1, keepdims=True)
    scale = lax.rsqrt(square * (1.0 / width) + 1e-05)
    for h in range(blocks):
        lanes = slice(h * chans, (h + 1) * chans)
        normed_out[:, lanes] = (mixed[h].astype(f32) * scale * gain[:, lanes]).astype(bf16)
    first, second = slots(routes_t[...], experts)
    pick = (first + second).astype(bf16).reshape(experts * CAP, rows)
    values = jnp.dot(pick, normed_out[...], preferred_element_type=f32).astype(bf16)
    _, size, _ = sent.shape
    copies = shards * size // (experts * CAP)
    if copies == 1:
        sent[...] = values.reshape(shards, size, width)
    else:
        for p in range(shards):
            e = p // copies
            sent[p] = values[e * CAP : (e + 1) * CAP, :]
    if len(send) == 1:
        send[0][...] = sent[...]
    else:
        for o in range(shards):
            send[o][...] = sent[at[0] ^ o]


def gates_kernel(normed, router, routes, gates):
    logits = jnp.dot(
        normed[...].astype(f32),
        router[...],
        precision=lax.Precision.HIGHEST,
        preferred_element_type=f32,
    )
    expert = lax.broadcasted_iota(jnp.int32, logits.shape, 1)
    for k in range(2):
        picked = jnp.where(routes[:, k : k + 1] == expert, logits, 0.0)
        value = jnp.sum(picked, axis=1, keepdims=True)
        gates[:, k : k + 1] = jax.nn.sigmoid(value)


def expert_kernel(count, owned, up, down, *refs):
    got, out, x = refs[:count], refs[-1 - count : -1], refs[-1]
    group = up.shape[0] // owned
    width = up.shape[1]
    for e in range(owned):
        pieces = []
        for piece in got:
            if len(piece.shape) == 2:
                pieces.append(piece[e * CAP : (e + 1) * CAP, :])
            else:
                slots = piece[:, e * CAP : (e + 1) * CAP, :]
                pieces.append(slots.reshape(piece.shape[0] * CAP, width))
        x[...] = jnp.concatenate(pieces, axis=0)
        total = jnp.zeros(x.shape, f32)
        for p in range(e * group, (e + 1) * group):
            hidden = jnp.dot(x[...], up[p], preferred_element_type=f32)
            hidden = jax.nn.gelu(hidden, approximate=True).astype(bf16)
            total = total + jnp.dot(hidden, down[p], preferred_element_type=f32)
        total = total.astype(bf16)
        rows = total.shape[0] // count
        for i, piece in enumerate(out):
            part = total[i * rows : (i + 1) * rows]
            if len(piece.shape) == 2:
                piece[e * CAP : (e + 1) * CAP, :] = part
            else:
                piece[:, e * CAP : (e + 1) * CAP, :] = part.reshape(piece.shape[0], CAP, width)


def run_experts(got, w_up, w_down, owned, after):
    width = got[0].shape[-1]
    slots = sum(math.prod(x.shape[:-1]) for x in got) // owned
    vmem = pl.BlockSpec(memory_space=pltpu.VMEM)
    return pl.pallas_call(
        functools.partial(expert_kernel, len(got), owned),
        out_shape=[jax.ShapeDtypeStruct(x.shape, x.dtype) for x in got],
        in_specs=[vmem] * (2 + len(got) + len(after)),
        out_specs=[vmem] * len(got),
        scratch_shapes=[pltpu.VMEM((slots, width), bf16)],
        compiler_params=params(),
        cost_estimate=pl.CostEstimate(flops=1, bytes_accessed=1, transcendentals=0),
        name="experts",
    )(w_up, w_down, *got, *after)


def combine_kernel(experts, blocks, shards, me, at, routes_t, gates, *refs):
    back, out, home = refs[: -blocks - 1], refs[-blocks - 1 : -1], refs[-1]
    _, size, width = home.shape
    rows = routes_t.shape[1]
    chans = width // blocks
    copies = shards * size // (experts * CAP)
    if len(back) == 1:
        home[...] = back[0][...]
    else:
        for o in range(shards):
            home[at[0] ^ o] = back[o][...]
    picks = slots(routes_t[...], experts)
    total = jnp.zeros((rows, width), f32)
    for k in range(2):
        pick = picks[k].astype(bf16).reshape(experts * CAP, rows)
        for c in range(copies):
            if copies == 1:
                values = home[...].reshape(experts * CAP, width)
            else:
                values = jnp.concatenate([home[e * copies + c] for e in range(experts)], axis=0)
            chosen = lax.dot_general(
                pick, values, (((0,), (0,)), ((), ())), preferred_element_type=f32
            )
            total = total + gates[:, k : k + 1] * chosen
    total = total.astype(bf16)
    parts = [total[:, h * chans : (h + 1) * chans] for h in range(blocks)]
    for o in range(blocks):
        value = parts[0]
        for h in range(1, blocks):
            value = jnp.where((me[0] ^ o) == h, parts[h], value)
        out[o][...] = value


def place_kernel(me, *refs):
    pieces, out, sems = refs[:-2], refs[-2], refs[-1]
    rows = pieces[0].shape[0]
    copies = []
    for o, piece in enumerate(pieces):
        start = pl.multiple_of((me[0] ^ o) * rows, rows)
        copies.append(pltpu.make_async_copy(piece, out.at[pl.ds(start, rows), :], sems.at[o]))
    for copy in copies:
        copy.start()
    for copy in copies:
        copy.wait()


def split(whole, me, count):
    shape = (whole.shape[0] // count, whole.shape[1])
    return pl.pallas_call(
        split_kernel,
        out_shape=[jax.ShapeDtypeStruct(shape, whole.dtype)] * count,
        in_specs=[pl.BlockSpec(memory_space=pltpu.SMEM), pl.BlockSpec(memory_space=pltpu.HBM)],
        out_specs=[pl.BlockSpec(memory_space=pltpu.VMEM)] * count,
        scratch_shapes=[pltpu.SemaphoreType.DMA((count,))],
        compiler_params=params(),
        name="split",
    )(me, whole)


def place(pieces, me):
    count, (rows, width) = len(pieces), pieces[0].shape
    return pl.pallas_call(
        place_kernel,
        out_shape=jax.ShapeDtypeStruct((count * rows, width), pieces[0].dtype),
        in_specs=[pl.BlockSpec(memory_space=pltpu.SMEM)]
        + [pl.BlockSpec(memory_space=pltpu.VMEM)] * count,
        out_specs=pl.BlockSpec(memory_space=pltpu.HBM),
        scratch_shapes=[pltpu.SemaphoreType.DMA((count,))],
        compiler_params=params(),
        name="place",
    )(me, *pieces)


def swap(pieces, axis, offsets, total):
    return [
        piece if o == 0 else lax.ppermute(piece, axis, [(i, i ^ o) for i in range(total)])
        for o, piece in zip(offsets, pieces)
    ]


def spread_out(block, axis):
    return lax.all_to_all(block, axis, split_axis=0, concat_axis=0, tiled=True)


def body(signal, gate_v, taps, skip, norm_gain, router, w_up, w_down, routes):
    tok, chans = signal.shape
    shards, blocks = lax.axis_size("ctx"), lax.axis_size("ch")
    per, rows, width = chans // shards, tok // blocks, chans * blocks
    experts = router.shape[1]
    parts = w_up.shape[0]
    owned = max(1, parts // 2)
    size = owned * CAP
    direct = 4 <= shards <= 8
    me = lax.axis_index("ch").astype(jnp.int32).reshape(1)
    at = lax.axis_index("ctx").astype(jnp.int32).reshape(1)
    shape = jax.ShapeDtypeStruct
    around = list(range(blocks))

    hbm = pl.BlockSpec(memory_space=pltpu.HBM)
    steps = max(1, chans // LANES)
    spread = pl.pallas_call(
        functools.partial(prep_kernel, shards),
        out_shape=shape((shards, 2 * per, tok), bf16),
        in_specs=[pl.BlockSpec(memory_space=pltpu.SMEM), hbm, hbm, hbm],
        out_specs=hbm,
        scratch_shapes=[
            pltpu.VMEM(signal.shape, signal.dtype),
            pltpu.VMEM(taps.shape, taps.dtype),
            pltpu.VMEM((1, chans), skip.dtype),
            pltpu.VMEM((shards, 2 * per, tok), bf16),
            pltpu.SemaphoreType.DMA((2 * steps + 1,)),
            pltpu.SemaphoreType.DMA((steps,)),
        ],
        compiler_params=params(FULL_LIMIT),
        name="prep",
    )(at, signal, taps, skip.reshape(1, chans))
    pieces = split(gate_v, me, blocks)
    turns = call(
        tables_kernel,
        [shape((shards, tok), f32)] * 2 + [shape((tok, tok), bf16)] * 2,
        [],
        [],
        "tables",
        [pltpu.VMEM((tok, tok), f32)] * 2,
    )
    got = spread_out(spread, "ctx")
    own, *pieces = swap(pieces, "ch", around, blocks)
    got, pieces = lax.optimization_barrier((got, pieces))
    pieces = [own, *pieces]
    conv = call(
        functools.partial(conv_kernel, blocks),
        shape((shards, blocks, per, rows), bf16),
        [],
        [got, *turns],
        "conv",
        [pltpu.VMEM((2 * shards * per, tok), bf16)] * 2 + [pltpu.VMEM((shards * per, tok), f32)] * 2,
    )
    conv = spread_out(conv.reshape(shards * blocks, per, rows), ("ctx", "ch"))
    conv = conv.reshape(shards, blocks, per, rows)
    routes_t = routes.T
    if direct:
        send_shape = [shape((size, width), bf16)] * shards
    else:
        send_shape = [shape((shards, size, width), bf16)]
    mixed_and_send = call(
        functools.partial(rows_kernel, experts, blocks),
        [shape((rows, chans), bf16)] * blocks + send_shape + [shape((rows, width), bf16)],
        [me, at],
        [routes_t, norm_gain.reshape(1, width), conv, *pieces],
        "rows",
        [pltpu.VMEM((blocks, rows, chans), bf16), pltpu.VMEM((shards, size, width), bf16)],
    )
    mixed, send, normed = mixed_and_send[:blocks], mixed_and_send[blocks:-1], mixed_and_send[-1]
    gates = call(gates_kernel, shape((rows, 2), f32), [], [normed, router, routes], "gates")
    if direct:
        done = run_experts(send[:1], w_up, w_down, owned, [])
        home = {0: done[0]}
        half = shards // 2
        cut = half + half // 2
        groups = [[*range(half, cut), *reversed(range(1, half))], list(range(cut, shards))]
        there = [swap([send[o] for o in group], "ctx", group, shards) for group in groups]
        for i, group in enumerate(groups):
            done = run_experts(there[i], w_up, w_down, owned, done[:1])
            home.update(zip(group, swap(done, "ctx", group, shards)))
        back = [home[o] for o in range(shards)]
        mixed, done = lax.optimization_barrier((mixed, done))
        mixed = swap(mixed, "ch", around, blocks)
    else:
        there = spread_out(send[0], "ctx")
        mixed = swap(mixed, "ch", around, blocks)
        (result,) = run_experts([there], w_up, w_down, owned, [])
        back = [spread_out(result, "ctx")]
    mixed = place(mixed, me)
    moe = call(
        functools.partial(combine_kernel, experts, blocks, shards),
        [shape((rows, chans), bf16)] * blocks,
        [me, at],
        [routes_t, gates, *back],
        "combine",
        [pltpu.VMEM((shards, size, width), bf16)],
    )
    moe = swap(moe, "ch", around, blocks)
    return (mixed, place(moe, me))


def solution(mesh):
    in_specs = (
        P("ctx", "ch"),
        P("ctx", "ch"),
        P("ctx", "ch"),
        P("ch"),
        P(),
        P(),
        P("ctx", None, None),
        P("ctx", None, None),
        P(("ctx", "ch"), None),
    )
    out_specs = (P("ctx", "ch"), P("ctx", "ch"))
    return jax.shard_map(body, mesh=mesh, in_specs=in_specs, out_specs=out_specs, check_vma=False)
```
